128 devices in a mesh: inst: 16 (over z, x), tp: 8 (over y, core).
Axes of the slice: x: 4, y: 4, z: 4, core: 2. Of those that a mesh axis runs over, the one named last changes fastest.
Arguments:
- queries: bfloat16 [128, 4, 64, 128], P('inst', None, 'tp'), may hold values from -90 to 90
- tail_keys: bfloat16 [128, 8, 256, 128], P('inst', 'tp'), may hold values from -5 to 5
- tail_values: bfloat16 [128, 8, 256, 128], P('inst', 'tp'), may hold values from -6 to 6
- new_keys: bfloat16 [128, 4, 8, 128], P('inst', None, 'tp'), may hold values from -2.5 to 2.5
- new_values: bfloat16 [128, 4, 8, 128], P('inst', None, 'tp'), may hold values from -6 to 6
- tail_lengths: int32 [128], P('inst'), may hold values from 1 to 256
- pool_keys: bfloat16 [768, 8, 256, 128], P('inst', 'tp'), may hold values from -5 to 5
- pool_values: bfloat16 [768, 8, 256, 128], P('inst', 'tp'), may hold values from -6 to 6
- slot_request: int32 [768], P('inst'), may hold values from 0 to 127, as said below
- out_weight: bfloat16 [8192, 8192], P('tp'), may hold values from -0.0625 to 0.0625
Outputs:
- projected: bfloat16 [128, 4, 8192], P('inst', None, 'tp')
The draws below stay inside these ranges and needn't reach their ends.
Inputs may be any that keep to these rules, and one draw needn't show every extreme that they name: `slot_request`: the 48 slots of one lender belong to 48 distinct requests; a request may have a slot on any lender or none.
All inputs are finite; a program needn't handle non-finite values.
Results may differ from the reference program's by a relative error of at most 0.019.
Values may be sent and summed in bfloat16 or wider, within the bound.
A program may use at most 128 MiB of HBM per device.

```python
import jax
import jax.numpy as jnp
from jax import lax

QH = 64
KVH = 8
HD = 128
D = 8192
BLOCK = 256
STEPS = 4
POOL = 48
REQUESTS = 128
SLOTS = 768
N_INST = 16


def owner_list(key):
    inner_key = jax.random.fold_in(key, 7)
    lender_keys = jax.random.split(inner_key, N_INST)
    picks = jax.vmap(lambda one_key: jax.random.permutation(one_key, REQUESTS)[:POOL])(lender_keys)
    return picks.reshape(SLOTS).astype(jnp.int32)


def query_base(key):
    inner_key = jax.random.fold_in(key, 11)
    return jnp.clip(jax.random.normal(inner_key, (REQUESTS, STEPS, QH, HD), jnp.float32), -4.5, 4.5)


def draw_queries(key, part):
    base_field = query_base(key)
    scaled = 16.0 * base_field
    return scaled.astype(jnp.bfloat16)


def draw_tail_keys(key, part):
    key = jax.random.fold_in(key, 2)
    key_field = 0.1 * jnp.clip(jax.random.normal(key, (REQUESTS, KVH, BLOCK, HD), jnp.float32), -4.5, 4.5)
    return key_field.astype(jnp.bfloat16)


def draw_pool_keys(key, part):
    key = jax.random.fold_in(key, 3)
    key_field = 0.1 * jnp.clip(jax.random.normal(key, (SLOTS, KVH, BLOCK, HD), jnp.float32), -4.5, 4.5)
    return key_field.astype(jnp.bfloat16)


def draw_slot_request(key, part):
    owners = owner_list(key)
    return owners


def touch_ends(array, stream_key, low, top_value):
    spot = [jax.random.randint(jax.random.fold_in(stream_key, axis), (), 0, length) for axis, length in enumerate(array.shape)]
    widest = array.shape.index(max(array.shape))
    neighbour = spot[:widest] + [(spot[widest] + 1) % array.shape[widest]] + spot[widest + 1:]
    return array.at[tuple(spot)].set(low).at[tuple(neighbour)].set(top_value)


def steps_of(rng, dims, cuts, least, largest):
    level = 1.0
    for dim, shards_of in cuts:
        steps = jax.random.uniform(jax.random.fold_in(jax.random.fold_in(rng, 6), dim), (shards_of,), jnp.float32, least / len(cuts), largest / len(cuts))
        level = level * jnp.repeat(jnp.exp(steps), dims[dim] // shards_of).reshape((-1,) + (1,) * (len(dims) - 1 - dim))
    return level


def gaussian(rng, extent, spread, limit, pieces=(), kind=jnp.bfloat16):
    gain = steps_of(rng, extent, pieces, -0.22, 0.18) if pieces else 1.0
    values = jax.random.normal(rng, extent, jnp.float32) * spread * gain
    return jnp.minimum(jnp.maximum(values, -limit), limit).astype(kind)


def setup_inputs(seed: int = 0) -> dict:
    keys = jax.random.split(jax.random.key(seed), 11)
    return {
        "queries": draw_queries(jax.random.fold_in(keys[10], 71), 0),
        "tail_keys": draw_tail_keys(jax.random.fold_in(keys[10], 71), 0),
        "tail_values": gaussian(keys[2], (REQUESTS, KVH, BLOCK, HD), 1.0, 6.0, ((0, 16), (1, 8))),
        "new_keys": gaussian(keys[3], (REQUESTS, STEPS, KVH, HD), 0.2, 2.5, ((0, 16), (2, 8))),
        "new_values": gaussian(keys[4], (REQUESTS, STEPS, KVH, HD), 1.0, 6.0, ((0, 16), (2, 8))),
        "tail_lengths": touch_ends(jax.random.randint(keys[5], (REQUESTS,), 1, BLOCK + 1), jax.random.fold_in(keys[5], 1), 1, BLOCK).astype(jnp.int32),
        "pool_keys": draw_pool_keys(jax.random.fold_in(keys[10], 71), 0),
        "pool_values": gaussian(keys[7], (SLOTS, KVH, BLOCK, HD), 1.0, 6.0, ((0, 16), (1, 8))),
        "slot_request": draw_slot_request(jax.random.fold_in(keys[10], 71), 0),
        "out_weight": gaussian(keys[9], (QH * HD, D), (QH * HD) ** -0.5, 0.0625, ((0, 8),)),
    }


VERY_LOW = -1e30


def softmax_parts(scores):
    row_peak = jnp.max(scores, axis=-1)
    exp_terms = jnp.exp(scores - row_peak[..., None])
    exp_total = jnp.sum(exp_terms, axis=-1)
    weights = lax.optimization_barrier(exp_terms.astype(jnp.bfloat16)).astype(jnp.float32)
    return row_peak, weights, exp_total


def lender_partial(all_queries, lender_keys, lender_values, owners):
    request_count, step_count, head_count, head_size = all_queries.shape
    slot_count, kv_heads = lender_keys.shape[0], lender_keys.shape[1]
    group_size = head_count // kv_heads
    query_rows = all_queries[owners].reshape(slot_count, step_count, kv_heads, group_size, head_size).astype(jnp.float32)
    scores = jnp.einsum("psvgd,pvtd->psvgt", query_rows, lender_keys.astype(jnp.float32)) * head_size ** -0.5
    row_peak, weights, exp_total = softmax_parts(scores)
    weighted_sum = jnp.einsum("psvgt,pvtd->psvgd", weights, lender_values.astype(jnp.float32))
    owner_mask = owners[None, :] == jnp.arange(request_count, dtype=jnp.int32)[:, None]
    best_peak = jnp.max(jnp.where(owner_mask[:, :, None, None, None], row_peak[None], VERY_LOW), axis=1)
    rescale = jnp.exp(row_peak - best_peak[owners])
    owner_matrix = owner_mask.astype(jnp.float32)
    denominator = jnp.dot(owner_matrix, (rescale * exp_total).reshape(slot_count, -1), precision=lax.Precision.HIGHEST).reshape(best_peak.shape)
    numerator = jnp.dot(owner_matrix, (rescale[..., None] * weighted_sum).reshape(slot_count, -1), precision=lax.Precision.HIGHEST).reshape(best_peak.shape + (head_size,))
    has_block = (jnp.sum(owner_matrix, axis=1) > 0.5)[:, None, None, None]
    safe_total = jnp.where(has_block, denominator, 1.0)
    partial_out = jnp.where(has_block[..., None], numerator / safe_total[..., None], 0.0)
    log_total = jnp.where(has_block, best_peak + jnp.log(safe_total), VERY_LOW)
    return partial_out, log_total


def local_partial(own_queries, tail_keys, tail_values, new_keys, new_values, tail_lengths):
    request_count, step_count, head_count, head_size = own_queries.shape
    kv_heads, block_len = tail_keys.shape[1], tail_keys.shape[2]
    group_size = head_count // kv_heads
    query_rows = own_queries.reshape(request_count, step_count, kv_heads, group_size, head_size).astype(jnp.float32)
    old_scores = jnp.einsum("rsvgd,rvtd->rsvgt", query_rows, tail_keys.astype(jnp.float32))
    new_scores = jnp.einsum("rsvgd,rjvd->rsvgj", query_rows, new_keys.astype(jnp.float32))
    scores = jnp.concatenate([old_scores, new_scores], axis=-1) * head_size ** -0.5
    old_valid = jnp.arange(block_len, dtype=jnp.int32)[None, :] < tail_lengths[:, None]
    new_valid = jnp.arange(step_count, dtype=jnp.int32)[None, :] <= jnp.arange(step_count, dtype=jnp.int32)[:, None]
    old_valid = jnp.broadcast_to(old_valid[:, None, None, None, :], old_scores.shape)
    new_valid = jnp.broadcast_to(new_valid[None, :, None, None, :], new_scores.shape)
    scores = jnp.where(jnp.concatenate([old_valid, new_valid], axis=-1), scores, VERY_LOW)
    row_peak, weights, exp_total = softmax_parts(scores)
    weighted_sum = jnp.einsum("rsvgt,rvtd->rsvgd", weights[..., :block_len], tail_values.astype(jnp.float32))
    weighted_sum = weighted_sum + jnp.einsum("rsvgj,rjvd->rsvgd", weights[..., block_len:], new_values.astype(jnp.float32))
    return weighted_sum / exp_total[..., None], row_peak + jnp.log(exp_total)


def reference(queries, tail_keys, tail_values, new_keys, new_values, tail_lengths, pool_keys, pool_values, slot_request, out_weight):
    local_out, local_log = local_partial(queries, tail_keys, tail_values, new_keys, new_values, tail_lengths)
    lender_keys = pool_keys.reshape((N_INST, POOL) + pool_keys.shape[1:])
    lender_values = pool_values.reshape((N_INST, POOL) + pool_values.shape[1:])
    lender_owners = slot_request.reshape(N_INST, POOL)

    def fold_step(running, lender_item):
        best_peak, numerator, denominator = running
        partial_out, log_total = lender_partial(queries, lender_item[0], lender_item[1], lender_item[2])
        next_peak = jnp.maximum(best_peak, log_total)
        keep_scale = jnp.exp(best_peak - next_peak)
        add_scale = jnp.exp(log_total - next_peak)
        numerator = numerator * keep_scale[..., None] + partial_out * add_scale[..., None]
        denominator = denominator * keep_scale + add_scale
        return (next_peak, numerator, denominator), None

    start_state = (local_log, local_out, jnp.ones_like(local_log))
    final_state, _ = lax.scan(fold_step, start_state, (lender_keys, lender_values, lender_owners))
    attention = (final_state[1] / final_state[2][..., None]).astype(jnp.bfloat16)
    flat_rows = attention.reshape(REQUESTS * STEPS, QH * HD)
    projected = jnp.dot(flat_rows, out_weight, preferred_element_type=jnp.float32)
    return projected.reshape(REQUESTS, STEPS, D).astype(jnp.bfloat16)
```

```python
import functools

import jax
import jax.numpy as jnp
from jax import lax
from jax.experimental import pallas as pl
from jax.experimental.pallas import tpu as pltpu
from jax.sharding import PartitionSpec as P

MESH = pl.DeviceIdType.MESH
VERY_LOW = -1e30
HD = 128
LOG2E = 1.4426950408889634
SCALE2 = HD**-0.5 * LOG2E
NT = (((1,), (1,)), ((), ()))
F32, BF16, I32 = jnp.float32, jnp.bfloat16, jnp.int32

SLOTS = 48
OWN = 8
REQ = 128
ROWS = 32
STAGES = 1
R = ROWS // STAGES
PR = OWN * R // 8
GROUP = 12


def remote(src, dst, send_sem, recv_sem, device):
    return pltpu.make_async_remote_copy(
        src_ref=src, dst_ref=dst, send_sem=send_sem, recv_sem=recv_sem, device_id=device, device_id_type=MESH
    )


def iota(shape, dim):
    return lax.broadcasted_iota(I32, shape, dim)


def to_rows(one_hot, columns):
    copies = jnp.concatenate([columns] * (128 // R), axis=0)
    high = copies.astype(BF16)
    rest = copies - high.astype(F32)
    middle = rest.astype(BF16)
    low = (rest - middle.astype(F32)).astype(BF16)
    parts = [lax.dot_general(one_hot, part, NT, preferred_element_type=F32) for part in (high, middle, low)]
    return parts[0] + parts[1] + parts[2]


def scaled_sum(weight_row, parts):
    n = len(parts)
    lane, row = iota((R, 128), 1), iota((R, 128), 0)
    picked = jnp.where(lane % R == row, jnp.broadcast_to(weight_row, (R, 128)), 0.0).astype(BF16)
    stacked = jnp.concatenate(parts, axis=0) if n > 1 else parts[0]
    return jnp.dot(picked[:, : n * R], stacked, preferred_element_type=F32)


def merge_weights(logs):
    top = functools.reduce(jnp.maximum, logs)
    terms = [jnp.exp2(log - top) for log in logs]
    total = functools.reduce(jnp.add, terms)
    inverse = 1.0 / total
    return [term * inverse for term in terms], top + jnp.log2(total)


def by_lane_group(weights):
    group = iota(weights[0].shape, 1) // R
    result = weights[0]
    for k in range(1, len(weights)):
        result = jnp.where(group == k, weights[k], result)
    return result


def kernel(
    sr, tl, q_hbm, tk_hbm, tv_hbm, nk_hbm, nv_hbm, pk_hbm, pv_hbm, w_hbm,
    out,
    qall, qown, kb, vb, tkb, tvb, nkb, nvb, wb,
    po, omsg, lmsg, ro1, rl1, m1, l1, ro2, rl2, lo, lloc, att, cs, cr, ys, yr,
    rho, ivec, inv,
    lsem, qsem, gs, gr, s1, r1, s2, r2, css, crs, yss, yrs,
):
    inst, tp = lax.axis_index("inst"), lax.axis_index("tp")
    z, x, y, c = inst // 4, inst % 4, tp // 2, tp % 2

    def along(half, axis, k):
        if (axis == 0) == (half == 0):
            return {"inst": ((z + k) % 4) * 4 + x}
        return {"inst": z * 4 + (x + k) % 4}

    def place(half):
        return (z, x) if half == 0 else (x, z)

    def local_copy(i, src, dst):
        copy = pltpu.make_async_copy(src, dst, lsem.at[i])
        copy.start()
        return copy

    c_qown = local_copy(0, q_hbm, qown)
    c_tk, c_tv = local_copy(1, tk_hbm, tkb), local_copy(2, tv_hbm, tvb)
    c_nk, c_nv = local_copy(3, nk_hbm, nkb), local_copy(4, nv_hbm, nvb)
    c_k, c_v = local_copy(5, pk_hbm, kb), local_copy(6, pv_hbm, vb)

    barrier = pltpu.get_barrier_semaphore()
    peers = [along(0, axis, k) for axis in (0, 1) for k in (1, 2, 3)]
    peers += [{"tp": y * 2 + 1 - c}] + [{"tp": ((y + k) % 4) * 2 + c} for k in (1, 2, 3)]
    for peer in peers:
        pl.semaphore_signal(barrier, inc=1, device_id=peer, device_id_type=MESH)
    pl.semaphore_wait(barrier, len(peers))

    sent = []

    def send(src, dst, ss, rs, device):
        copy = remote(src, dst, ss, rs, device)
        copy.start()
        sent.append(copy)

    def chunk(half, dp, dq):
        p, q = place(half)
        return pl.ds(half * 64 + (((p + dp) % 4) * 4 + (q + dq) % 4) * 4, 4)

    own_copies = []
    for s in range(STAGES):
        for axis in (0, 1):
            for k in (2, 1, 3):
                for half in (0, 1):
                    back = (4 - k) % 4
                    sem = gr.at[s, half, back, 0] if axis == 0 else gr.at[s, half, 0, back]
                    send(
                        q_hbm.at[pl.ds(4 * half, 4), pl.ds(s * R, R)],
                        qall.at[s, chunk(half, 0, 0)],
                        gs.at[s, half, axis * 3 + k - 1],
                        sem,
                        along(half, axis, k),
                    )
        for half in (0, 1):
            copy = pltpu.make_async_copy(
                q_hbm.at[pl.ds(4 * half, 4), pl.ds(s * R, R)], qall.at[s, chunk(half, 0, 0)], qsem.at[s, half]
            )
            copy.start()
            own_copies.append(copy)
    c_w = local_copy(7, w_hbm, wb)

    def gathered(s, half, dp, dq):
        ref = qall.at[s, chunk(half, dp, dq)]
        remote(ref, ref, gs.at[s, half, 0], gr.at[s, half, dp, dq], along(half, 0, 1)).wait_recv()

    def forward(s):
        for dp in (3, 1, 2):
            for half in (0, 1):
                gathered(s, half, dp, 0)
                for k in (2, 1, 3):
                    ref = qall.at[s, chunk(half, dp, 0)]
                    send(ref, ref, gs.at[s, half, 3 + dp * 3 + k - 1], gr.at[s, half, dp, (4 - k) % 4], along(half, 1, k))

    lane8 = iota((8, 128), 1)
    at_slot = jnp.full((8, 128), -1, I32)
    slot_of = jnp.full((8, 128), SLOTS, I32)
    for j in range(SLOTS):
        request = sr[j]
        home, half, fourth = request // 8, (request % 8) // 4, request % 4
        swapped = (home % 4) * 4 + home // 4
        position = half * 64 + jnp.where(half == 0, home, swapped) * 4 + fourth
        rho[j] = position
        at_slot = jnp.where(lane8 == j, position, at_slot)
        slot_of = jnp.where(lane8 == position, j, slot_of)
    ivec[...] = slot_of
    c_inv = pltpu.make_async_copy(ivec, inv, lsem.at[8])
    c_inv.start()
    one_hot = (jnp.broadcast_to(at_slot[0:1], (REQ, 128)) == iota((REQ, 128), 0)).astype(F32)
    missing = (jnp.sum(one_hot, axis=1, keepdims=True) - 1.0) * (-VERY_LOW)
    one_hot = one_hot.astype(BF16)
    for s in range(STAGES):
        po[s, SLOTS] = jnp.zeros((R, HD), BF16)
    l1[...] = jnp.zeros_like(l1)
    lloc[...] = jnp.zeros_like(lloc)

    for s in range(STAGES):
        forward(s)

    c_qown.wait()
    c_tk.wait()
    c_tv.wait()
    c_nk.wait()
    c_nv.wait()
    new_scores = lax.dot_general(qown[...].reshape(OWN * ROWS, HD), nkb[...], NT, preferred_element_type=F32)
    token = iota((ROWS, 256), 1)
    new_lane, step = iota((ROWS, 32), 1), iota((ROWS, 32), 0) // 8
    lane, log_columns = iota((ROWS, 128), 1), jnp.zeros((ROWS, 128), F32)
    for r in range(OWN):
        old = lax.dot_general(qown[r], tkb[r], NT, preferred_element_type=F32)
        old = jnp.where(token < tl[r], old, VERY_LOW)
        new = new_scores[r * ROWS : (r + 1) * ROWS]
        new = jnp.where((new_lane >= 4 * r) & (new_lane <= 4 * r + step), new, VERY_LOW)
        peak = jnp.maximum(jnp.max(old, axis=1, keepdims=True), jnp.max(new, axis=1, keepdims=True))
        old = jnp.exp2((old - peak) * SCALE2)
        new = jnp.exp2((new - peak) * SCALE2)
        total = jnp.sum(old, axis=1, keepdims=True) + jnp.sum(new, axis=1, keepdims=True)
        result = jnp.dot(old.astype(BF16), tvb[r], preferred_element_type=F32)
        result = result + jnp.dot(new.astype(BF16), nvb[...], preferred_element_type=F32)
        lo[r] = (result * (1.0 / total)).astype(BF16)
        log_columns = jnp.where(lane == r, peak * SCALE2 + jnp.log2(total), log_columns)
    pick = (iota((OWN, 128), 0) == iota((OWN, 128), 1)).astype(F32).astype(BF16)
    for s in range(STAGES):
        rows = to_rows(pick, log_columns[s * R : (s + 1) * R])
        lloc[s, 0, 0:4] = rows[0:4]
        lloc[s, 1, 0:4] = rows[4:8]

    c_inv.wait()
    for copy in own_copies:
        copy.wait()

    def lend(s):
        lane = iota((R, 128), 1)

        def group(g, log_columns):
            scores = []
            for u in range(GROUP):
                j = g * GROUP + u
                scores.append(lax.dot_general(qall[s, rho[j]], kb[j], NT, preferred_element_type=F32))
            peaks = [jnp.max(score, axis=1, keepdims=True) for score in scores]
            terms = [jnp.exp2((score - peak) * SCALE2) for score, peak in zip(scores, peaks)]
            totals = [jnp.sum(term, axis=1, keepdims=True) for term in terms]
            for u in range(GROUP):
                j = g * GROUP + u
                result = jnp.dot(terms[u].astype(BF16), vb[j], preferred_element_type=F32)
                po[s, j] = (result * (1.0 / totals[u])).astype(BF16)
                log_columns = jnp.where(lane == j, peaks[u] * SCALE2 + jnp.log2(totals[u]), log_columns)
            return log_columns

        log_columns = lax.fori_loop(0, SLOTS // GROUP, group, jnp.zeros((R, 128), F32))
        lmsg[s] = to_rows(one_hot, log_columns) + missing

        def reorder(i, carry):
            for u in range(16):
                n = i * 16 + u
                omsg[s, n] = po[s, inv[0, n]]
            return carry

        lax.fori_loop(0, REQ // 16, reorder, 0)
        for k in (2, 1, 3):
            for half in (0, 1):
                p, _ = place(half)
                part = pl.ds(pl.multiple_of(half * 64 + ((p + k) % 4) * 16, 16), 16)
                to = along(half, 0, k)
                send(lmsg.at[s, part], rl1.at[s, half, k - 1], s1.at[s, half, k - 1, 0], r1.at[s, half, k - 1, 0], to)
                send(omsg.at[s, part], ro1.at[s, half, k - 1], s1.at[s, half, k - 1, 1], r1.at[s, half, k - 1, 1], to)

    def first_merge(s, half):
        p, q = place(half)
        base = pl.multiple_of(half * 64 + p * 16, 16)
        for k in (1, 3, 2):
            remote(rl1.at[s, half, k - 1], rl1.at[s, half, k - 1], s1.at[s, half, 0, 0], r1.at[s, half, k - 1, 0], along(half, 0, k)).wait_recv()
        logs = [lmsg[s, pl.ds(base, 16)]] + [rl1[s, half, k] for k in range(3)]
        weights, log = merge_weights(logs)
        weights = by_lane_group(weights)
        for i in range(4):
            l1[s, half, i, 0:4] = log[4 * i : 4 * i + 4]
        for k in (1, 3, 2):
            remote(ro1.at[s, half, k - 1], ro1.at[s, half, k - 1], s1.at[s, half, 0, 0], r1.at[s, half, k - 1, 1], along(half, 0, k)).wait_recv()
        for i in range(16):
            parts = [omsg[s, base + i]] + [ro1[s, half, k, i] for k in range(3)]
            m1[s, half, i] = scaled_sum(weights[i : i + 1], parts).astype(BF16)
        for k in (2, 1, 3):
            other = (q + k) % 4
            to = along(half, 1, k)
            send(l1.at[s, half, other], rl2.at[s, half, k - 1], s2.at[s, half, k - 1, 0], r2.at[s, half, k - 1, 0], to)
            send(m1.at[s, half, pl.ds(other * 4, 4)], ro2.at[s, half, k - 1], s2.at[s, half, k - 1, 1], r2.at[s, half, k - 1, 1], to)

    def second_merge(s, half):
        _, q = place(half)
        for k in (1, 3, 2):
            remote(rl2.at[s, half, k - 1], rl2.at[s, half, k - 1], s2.at[s, half, 0, 0], r2.at[s, half, k - 1, 0], along(half, 1, k)).wait_recv()
            remote(ro2.at[s, half, k - 1], ro2.at[s, half, k - 1], s2.at[s, half, 0, 0], r2.at[s, half, k - 1, 1], along(half, 1, k)).wait_recv()
        logs = [l1[s, half, q]] + [rl2[s, half, k] for k in range(3)] + [lloc[s, half]]
        weights, _ = merge_weights(logs)
        lent, home = by_lane_group(weights[:4]), weights[4]
        for i in range(4):
            parts = [m1[s, half, q * 4 + i]] + [ro2[s, half, k, i] for k in range(3)]
            r = half * 4 + i
            result = scaled_sum(lent[i : i + 1], parts)
            result = result + scaled_sum(home[i : i + 1], [lo[r, s * R : (s + 1) * R]])
            att[s, r * R : (r + 1) * R] = result

    def project(s):
        heads = [att[s, pl.ds(h, PR, stride=8)].astype(BF16) for h in range(8)]
        flat = jnp.concatenate(heads, axis=1)

        def columns(target):
            at = pl.multiple_of(target * 1024, 1024)
            return jnp.dot(flat, wb[:, pl.ds(at, 1024)], preferred_element_type=F32)

        for dy in (2, 1, 3, 0):
            cs[s, dy] = columns(((y + dy) % 4) * 2 + 1 - c).astype(BF16)
            send(cs.at[s, dy], cr.at[s, dy], css.at[s, dy], crs.at[s, dy], {"tp": y * 2 + 1 - c})
        mine = None
        for dy in (2, 1, 3, 0):
            value = columns(((y + dy) % 4) * 2 + c)
            remote(cr.at[s, dy], cr.at[s, dy], css.at[s, dy], crs.at[s, dy], {"tp": y * 2 + 1 - c}).wait_recv()
            value = value + cr[s, dy].astype(F32)
            if dy:
                ys[s, dy - 1] = value.astype(BF16)
                send(ys.at[s, dy - 1], yr.at[s, dy - 1], yss.at[s, dy - 1], yrs.at[s, dy - 1], {"tp": ((y + dy) % 4) * 2 + c})
            else:
                mine = value
        return mine

    def finish(s, value):
        for dy in (1, 3, 2):
            remote(yr.at[s, dy - 1], yr.at[s, dy - 1], yss.at[s, dy - 1], yrs.at[s, dy - 1], {"tp": ((y + dy) % 4) * 2 + c}).wait_recv()
            value = value + yr[s, dy - 1].astype(F32)
        out[s] = value.astype(BF16)

    for s in range(STAGES):
        for half in (0, 1):
            for dp in (0, 1, 3, 2):
                for dq in (1, 3, 2):
                    gathered(s, half, dp, dq)
        if s == 0:
            c_k.wait()
            c_v.wait()
        lend(s)
    for s in range(STAGES):
        for half in (0, 1):
            first_merge(s, half)
    for s in range(STAGES):
        for half in (0, 1):
            second_merge(s, half)
        if s == 0:
            c_w.wait()
        mine = project(s)
        finish(s, mine)
    for copy in sent:
        copy.wait_send()


def per_device(
    queries, tail_keys, tail_values, new_keys, new_values, tail_lengths, pool_keys, pool_values, slot_request, out_weight
):
    any_space = pl.BlockSpec(memory_space=pl.ANY)
    smem = pl.BlockSpec(memory_space=pltpu.SMEM)
    dma = pltpu.SemaphoreType.DMA
    S = STAGES

    def v(*shape, dtype=BF16):
        return pltpu.VMEM(shape, dtype)

    result = pl.pallas_call(
        kernel,
        out_shape=jax.ShapeDtypeStruct((S, PR, 1024), BF16),
        in_specs=[smem, smem] + [any_space] * 8,
        out_specs=pl.BlockSpec(memory_space=pltpu.VMEM),
        scratch_shapes=[
            v(S, REQ, R, HD), v(OWN, ROWS, HD), v(SLOTS, 256, HD), v(SLOTS, 256, HD), v(OWN, 256, HD), v(OWN, 256, HD),
            v(32, HD), v(32, HD), v(1024, 8192),
            v(S, SLOTS + 1, R, HD), v(S, REQ, R, HD), v(S, REQ, 128, dtype=F32),
            v(S, 2, 3, 16, R, HD), v(S, 2, 3, 16, 128, dtype=F32),
            v(S, 2, 16, R, HD), v(S, 2, 4, 8, 128, dtype=F32),
            v(S, 2, 3, 4, R, HD), v(S, 2, 3, 8, 128, dtype=F32),
            v(OWN, ROWS, HD), v(S, 2, 8, 128, dtype=F32), v(S, OWN * R, HD, dtype=F32),
            v(S, 4, PR, 1024), v(S, 4, PR, 1024), v(S, 3, PR, 1024), v(S, 3, PR, 1024),
            pltpu.SMEM((SLOTS,), I32), v(8, 128, dtype=I32), pltpu.SMEM((8, 128), I32),
            dma((9,)), dma((S, 2)), dma((S, 2, 15)), dma((S, 2, 4, 4)),
            dma((S, 2, 3, 2)), dma((S, 2, 3, 2)), dma((S, 2, 3, 2)), dma((S, 2, 3, 2)),
            dma((S, 4)), dma((S, 4)), dma((S, 3)), dma((S, 3)),
        ],
        name="lent_attention",
        compiler_params=pltpu.CompilerParams(collective_id=0, has_side_effects=True, vmem_limit_bytes=50 * 2**20),
    )(
        slot_request,
        tail_lengths,
        queries.reshape(OWN, ROWS, HD),
        tail_keys.reshape(OWN, 256, HD),
        tail_values.reshape(OWN, 256, HD),
        new_keys.reshape(32, HD),
        new_values.reshape(32, HD),
        pool_keys.reshape(SLOTS, 256, HD),
        pool_values.reshape(SLOTS, 256, HD),
        out_weight,
    )
    result = result.reshape(S, OWN, 4 // S, 1024)
    return result.transpose(1, 0, 2, 3).reshape(OWN, 4, 1024)


def solution(mesh):
    placed = (
        P("inst", None, "tp", None),
        P("inst", "tp", None, None),
        P("inst", "tp", None, None),
        P("inst", None, "tp", None),
        P("inst", None, "tp", None),
        P("inst"),
        P("inst", "tp", None, None),
        P("inst", "tp", None, None),
        P("inst"),
        P("tp", None),
    )
    return jax.shard_map(
        per_device, mesh=mesh, in_specs=placed, out_specs=P("inst", None, "tp"), check_vma=False
    )
```

```python
import functools

import jax
import jax.numpy as jnp
from jax import lax
from jax.experimental import pallas as pl
from jax.experimental.pallas import tpu as pltpu
from jax.sharding import PartitionSpec as P

MESH = pl.DeviceIdType.MESH
VERY_LOW = -1e30
HD = 128
LOG2E = 1.4426950408889634
SCALE2 = HD**-0.5 * LOG2E
NT = (((1,), (1,)), ((), ()))
F32, BF16, I32 = jnp.float32, jnp.bfloat16, jnp.int32

SLOTS = 48
OWN = 8
REQ = 128
R = 32
PAIRS = 16
FORWARD = (2, 3, 1)
FIRST = (2, 1, 3)


def remote(src, dst, send_sem, recv_sem, device):
    return pltpu.make_async_remote_copy(
        src_ref=src, dst_ref=dst, send_sem=send_sem, recv_sem=recv_sem, device_id=device, device_id_type=MESH
    )


def iota(shape, dim):
    return lax.broadcasted_iota(I32, shape, dim)


def to_rows(one_hot, columns):
    copies = jnp.concatenate([columns] * (128 // R), axis=0)
    high = copies.astype(BF16)
    rest = copies - high.astype(F32)
    middle = rest.astype(BF16)
    low = (rest - middle.astype(F32)).astype(BF16)
    parts = [lax.dot_general(one_hot, part, NT, preferred_element_type=F32) for part in (high, middle, low)]
    return parts[0] + parts[1] + parts[2]


def scaled_sums(weights, parts):
    lane, row = iota((R, 128), 1), iota((R, 128), 0)
    diagonal = lane % R == row
    zeros = jnp.zeros((R, 128), BF16)
    picked = [jnp.where(diagonal, jnp.broadcast_to(weights[i : i + 1], (R, 128)), 0.0).astype(BF16) for i in range(4)]
    rows = [jnp.concatenate([zeros, pick] if i % 2 else [pick, zeros], axis=1) for i, pick in enumerate(picked)]
    left = jnp.concatenate(parts[0] + parts[1], axis=0)
    right = jnp.concatenate(parts[2] + parts[3], axis=0)
    result = jnp.dot(jnp.concatenate(rows, axis=0), jnp.concatenate([left, right], axis=1), preferred_element_type=F32)
    return [result[i * R : (i + 1) * R, (i // 2) * 128 : (i // 2 + 1) * 128] for i in range(4)]


def merge_weights(logs):
    top = functools.reduce(jnp.maximum, logs)
    terms = [jnp.exp2(log - top) for log in logs]
    total = functools.reduce(jnp.add, terms)
    inverse = 1.0 / total
    return [term * inverse for term in terms], top + jnp.log2(total)


def by_lane_group(weights):
    group = iota(weights[0].shape, 1) // R
    result = weights[0]
    for k in range(1, len(weights)):
        result = jnp.where(group == k, weights[k], result)
    return result


def kernel(
    sr_hbm, tl_hbm, q_hbm, tk_hbm, tv_hbm, nk_hbm, nv_hbm, pk_hbm, pv_hbm, w_hbm,
    out,
    qall, qown, kb, vb, tkb, tvb, nkb, nvb, wb,
    omsg, lmsg, absent, ro1, rl1, m1, l1, ro2, rl2, lo, lloc, att, cs, cr, ys, yr,
    sr, tl, ivec, inv,
    lsem, qsem, gs, gr, s1, r1, s2, r2, css, crs, yss, yrs,
):
    inst, tp = lax.axis_index("inst"), lax.axis_index("tp")
    z, x, y, c = inst // 4, inst % 4, tp // 2, tp % 2

    def along(half, axis, k):
        if (axis == 0) == (half == 0):
            return {"inst": ((z + k) % 4) * 4 + x}
        return {"inst": z * 4 + (x + k) % 4}

    def place(half):
        return (z, x) if half == 0 else (x, z)

    barrier = pltpu.get_barrier_semaphore()
    peers = [along(0, axis, k) for axis in (0, 1) for k in (2, 1, 3)]
    peers += [{"tp": ((y + k) % 4) * 2 + c} for k in (2, 1, 3)] + [{"tp": y * 2 + 1 - c}]
    for peer in peers:
        pl.semaphore_signal(barrier, inc=1, device_id=peer, device_id_type=MESH)

    def local_copy(i, src, dst):
        copy = pltpu.make_async_copy(src, dst, lsem.at[i])
        copy.start()
        return copy

    c_sr, c_tl = local_copy(9, sr_hbm, sr), local_copy(10, tl_hbm, tl)
    c_qown = local_copy(0, q_hbm, qown)
    c_k, c_v = local_copy(5, pk_hbm, kb), local_copy(6, pv_hbm, vb)
    pl.semaphore_wait(barrier, len(peers))

    sent = []

    def send(src, dst, ss, rs, device):
        copy = remote(src, dst, ss, rs, device)
        copy.start()
        sent.append(copy)

    def received(dst, ss, rs):
        remote(dst, dst, ss, rs, along(0, 0, 1)).wait_recv()

    def chunk(half, dp, dq):
        p, q = place(half)
        return pl.ds(half * 64 + (((p + dp) % 4) * 4 + (q + dq) % 4) * 4, 4)

    for axis in (0, 1):
        for k in (2, 1, 3):
            for half in (0, 1):
                back = (4 - k) % 4
                send(
                    q_hbm.at[pl.ds(4 * half, 4)],
                    qall.at[chunk(half, 0, 0)],
                    gs.at[half, axis * 3 + k - 1],
                    gr.at[half, back, 0] if axis == 0 else gr.at[half, 0, back],
                    along(half, axis, k),
                )
    own_copies = []
    for half in (0, 1):
        copy = pltpu.make_async_copy(q_hbm.at[pl.ds(4 * half, 4)], qall.at[chunk(half, 0, 0)], qsem.at[half])
        copy.start()
        own_copies.append(copy)
    c_tk, c_tv = local_copy(1, tk_hbm, tkb), local_copy(2, tv_hbm, tvb)
    c_nk, c_nv = local_copy(3, nk_hbm, nkb), local_copy(4, nv_hbm, nvb)
    c_w = local_copy(7, w_hbm, wb)

    def gathered(half, dp, dq):
        received(qall.at[chunk(half, dp, dq)], gs.at[half, 0], gr.at[half, dp, dq])

    def forward(dp):
        for half in (0, 1):
            gathered(half, dp, 0)
            for k in (2, 1, 3):
                ref = qall.at[chunk(half, dp, 0)]
                send(ref, ref, gs.at[half, 3 + dp * 3 + k - 1], gr.at[half, dp, (4 - k) % 4], along(half, 1, k))

    c_sr.wait()
    c_tl.wait()
    lane8 = iota((8, 128), 1)
    at_slot = jnp.full((8, 128), -1, I32)
    slot_of = jnp.zeros((8, 128), I32)
    for j in range(SLOTS):
        request = sr[j]
        home, half, fourth = request // 8, (request % 8) // 4, request % 4
        swapped = (home % 4) * 4 + home // 4
        position = half * 64 + jnp.where(half == 0, home, swapped) * 4 + fourth
        at_slot = jnp.where(lane8 == j, position, at_slot)
        slot_of = jnp.where(lane8 == position, j, slot_of)
    ivec[...] = slot_of
    c_inv = pltpu.make_async_copy(ivec, inv, lsem.at[8])
    c_inv.start()
    here = (jnp.broadcast_to(at_slot[0:1], (REQ, 128)) == iota((REQ, 128), 0)).astype(F32)
    absent[...] = jnp.broadcast_to((1.0 - jnp.sum(here, axis=1, keepdims=True)) * VERY_LOW, (REQ, 128))
    l1[...] = jnp.zeros_like(l1)
    lloc[...] = jnp.zeros_like(lloc)

    def home_part():
        c_qown.wait()
        c_tk.wait()
        c_tv.wait()
        c_nk.wait()
        c_nv.wait()
        new_scores = lax.dot_general(qown[...].reshape(OWN * R, HD), nkb[...], NT, preferred_element_type=F32)
        token = iota((R, 256), 1)
        new_lane, step = iota((R, 32), 1), iota((R, 32), 0) // 8
        lane, log_columns = iota((R, 128), 1), jnp.zeros((R, 128), F32)
        for r in range(OWN):
            old = lax.dot_general(qown[r], tkb[r], NT, preferred_element_type=F32)
            old = jnp.where(token < tl[r], old, VERY_LOW)
            new = new_scores[r * R : (r + 1) * R]
            new = jnp.where((new_lane >= 4 * r) & (new_lane <= 4 * r + step), new, VERY_LOW)
            peak = jnp.maximum(jnp.max(old, axis=1, keepdims=True), jnp.max(new, axis=1, keepdims=True))
            old = jnp.exp2((old - peak) * SCALE2)
            new = jnp.exp2((new - peak) * SCALE2)
            total = jnp.sum(old, axis=1, keepdims=True) + jnp.sum(new, axis=1, keepdims=True)
            result = jnp.dot(old.astype(BF16), tvb[r], preferred_element_type=F32)
            result = result + jnp.dot(new.astype(BF16), nvb[...], preferred_element_type=F32)
            lo[r] = (result * (1.0 / total)).astype(BF16)
            log_columns = jnp.where(lane == r, peak * SCALE2 + jnp.log2(total), log_columns)
        pick = (iota((OWN, 128), 0) == iota((OWN, 128), 1)).astype(F32).astype(BF16)
        rows = to_rows(pick, log_columns)
        lloc[0, 0:4] = rows[0:4]
        lloc[1, 0:4] = rows[4:8]

    def lend(dp):
        lane, zeros = iota((R, 128), 1), jnp.zeros((R, HD), BF16)
        bases = []
        for half in (0, 1):
            p, _ = place(half)
            bases.append(pl.multiple_of(half * 64 + ((p + dp) % 4) * 16, 16))
        log_columns = [jnp.zeros((R, 128), F32)] * 2
        todo = [(half, i) for half in (0, 1) for i in range(0, 16, 2)]
        for first in range(0, len(todo), PAIRS):
            batch = todo[first : first + PAIRS]
            slots = [[inv[0, bases[half] + i + u] for u in (0, 1)] for half, i in batch]
            scores = []
            for (half, i), (a, b) in zip(batch, slots):
                queries = [qall[bases[half] + i + u] for u in (0, 1)]
                queries = [jnp.concatenate([queries[0], zeros], axis=1), jnp.concatenate([zeros, queries[1]], axis=1)]
                keys = jnp.concatenate([kb[a], kb[b]], axis=1)
                scores.append(lax.dot_general(jnp.concatenate(queries, axis=0), keys, NT, preferred_element_type=F32))
            peaks = [jnp.max(score, axis=1, keepdims=True) for score in scores]
            terms = [jnp.exp2((score - peak) * SCALE2) for score, peak in zip(scores, peaks)]
            totals = [jnp.sum(term, axis=1, keepdims=True) for term in terms]
            for (half, i), (a, b), peak, term, total in zip(batch, slots, peaks, terms, totals):
                values = jnp.concatenate([vb[a], vb[b]], axis=1)
                result = jnp.dot(term.astype(BF16), values, preferred_element_type=F32)
                inverse = 1.0 / total
                logs = peak * SCALE2 + jnp.log2(total)
                omsg[bases[half] + i] = (result[:R, :HD] * inverse[:R]).astype(BF16)
                omsg[bases[half] + i + 1] = (result[R:, HD:] * inverse[R:]).astype(BF16)
                log_columns[half] = jnp.where(lane == i, logs[:R], log_columns[half])
                log_columns[half] = jnp.where(lane == i + 1, logs[R:], log_columns[half])
        pick = (iota((16, 128), 0) == iota((16, 128), 1)).astype(F32).astype(BF16)
        for half in (0, 1):
            part = pl.ds(bases[half], 16)
            lmsg[part] = to_rows(pick, log_columns[half]) + absent[part]
            if dp:
                to = along(half, 0, dp)
                send(omsg.at[part], ro1.at[half, dp - 1], s1.at[half, dp - 1, 1], r1.at[half, dp - 1, 1], to)
                send(lmsg.at[part], rl1.at[half, dp - 1], s1.at[half, dp - 1, 0], r1.at[half, dp - 1, 0], to)

    def first_merge(half):
        p, q = place(half)
        base = pl.multiple_of(half * 64 + p * 16, 16)
        for k in FIRST:
            received(rl1.at[half, k - 1], s1.at[half, 0, 0], r1.at[half, k - 1, 0])
            received(ro1.at[half, k - 1], s1.at[half, 0, 0], r1.at[half, k - 1, 1])
        weights, log = merge_weights([lmsg[pl.ds(base, 16)]] + [rl1[half, k] for k in range(3)])
        weights = by_lane_group(weights)
        for i in range(4):
            l1[half, i, 0:4] = log[4 * i : 4 * i + 4]
        for i in range(0, 16, 4):
            parts = [[omsg[base + i + u]] + [ro1[half, k, i + u] for k in range(3)] for u in range(4)]
            for u, result in enumerate(scaled_sums(weights[i : i + 4], parts)):
                m1[half, i + u] = result.astype(BF16)
        for k in (2, 1, 3):
            other = (q + k) % 4
            to = along(half, 1, k)
            send(m1.at[half, pl.ds(other * 4, 4)], ro2.at[half, k - 1], s2.at[half, k - 1, 1], r2.at[half, k - 1, 1], to)
            send(l1.at[half, other], rl2.at[half, k - 1], s2.at[half, k - 1, 0], r2.at[half, k - 1, 0], to)

    def second_merge(half):
        _, q = place(half)
        for k in (1, 3, 2):
            received(rl2.at[half, k - 1], s2.at[half, 0, 0], r2.at[half, k - 1, 0])
            received(ro2.at[half, k - 1], s2.at[half, 0, 0], r2.at[half, k - 1, 1])
        weights, _ = merge_weights([l1[half, q]] + [rl2[half, k] for k in range(3)] + [lloc[half]])
        lent, home = by_lane_group(weights[:4]), weights[4]
        parts = [[m1[half, q * 4 + u]] + [ro2[half, k, u] for k in range(3)] for u in range(4)]
        lane, row = iota((R, 128), 1), iota((R, 128), 0)
        picked = [
            jnp.where(lane == row + u * R, jnp.broadcast_to(home[u : u + 1], (R, 128)), 0.0).astype(BF16) for u in range(4)
        ]
        homes = jnp.concatenate([lo[half * 4 + u] for u in range(4)], axis=0)
        own = jnp.dot(jnp.concatenate(picked, axis=0), homes, preferred_element_type=F32)
        for u, result in enumerate(scaled_sums(lent[0:4], parts)):
            att[(half * 4 + u) * R : (half * 4 + u + 1) * R] = result + own[u * R : (u + 1) * R]

    order = (0,) + FORWARD
    home_part()
    for dp in FORWARD:
        forward(dp)
    c_inv.wait()
    for copy in own_copies:
        copy.wait()
    for dp in order:
        for half in (0, 1):
            for dq in (1, 3, 2):
                gathered(half, dp, dq)
        if dp == 0:
            c_k.wait()
            c_v.wait()
        lend(dp)
    for half in (0, 1):
        first_merge(half)
    for half in (0, 1):
        second_merge(half)

    flat = jnp.concatenate([att[pl.ds(h, R, stride=8)].astype(BF16) for h in range(8)], axis=1)
    c_w.wait()

    def columns(target):
        return jnp.dot(flat, wb[:, pl.ds(pl.multiple_of(target * 1024, 1024), 1024)], preferred_element_type=F32)

    for dy in (2, 1, 3, 0):
        cs[dy] = columns(((y + dy) % 4) * 2 + 1 - c).astype(BF16)
        send(cs.at[dy], cr.at[dy], css.at[dy], crs.at[dy], {"tp": y * 2 + 1 - c})
    value = None
    for dy in (2, 1, 3, 0):
        value = columns(((y + dy) % 4) * 2 + c)
        received(cr.at[dy], css.at[dy], crs.at[dy])
        value = value + cr[dy].astype(F32)
        if dy:
            ys[dy - 1] = value.astype(BF16)
            send(ys.at[dy - 1], yr.at[dy - 1], yss.at[dy - 1], yrs.at[dy - 1], {"tp": ((y + dy) % 4) * 2 + c})
    for dy in (2, 1, 3):
        received(yr.at[dy - 1], yss.at[dy - 1], yrs.at[dy - 1])
        value = value + yr[dy - 1].astype(F32)
    out[...] = value.astype(BF16)
    for copy in sent:
        copy.wait_send()


def per_device(
    queries, tail_keys, tail_values, new_keys, new_values, tail_lengths, pool_keys, pool_values, slot_request, out_weight
):
    in_hbm = pl.BlockSpec(memory_space=pltpu.HBM)
    dma = pltpu.SemaphoreType.DMA

    def v(*shape, dtype=BF16):
        return pltpu.VMEM(shape, dtype)

    args = (
        slot_request,
        tail_lengths,
        queries.reshape(OWN, R, HD),
        tail_keys.reshape(OWN, 256, HD),
        tail_values.reshape(OWN, 256, HD),
        new_keys.reshape(R, HD),
        new_values.reshape(R, HD),
        pool_keys.reshape(SLOTS, 256, HD),
        pool_values.reshape(SLOTS, 256, HD),
        out_weight,
    )
    result = pl.pallas_call(
        kernel,
        out_shape=jax.ShapeDtypeStruct((R, 1024), BF16),
        in_specs=[in_hbm] * len(args),
        out_specs=pl.BlockSpec(memory_space=pltpu.VMEM),
        scratch_shapes=[
            v(REQ, R, HD), v(OWN, R, HD), v(SLOTS, 256, HD), v(SLOTS, 256, HD), v(OWN, 256, HD), v(OWN, 256, HD),
            v(R, HD), v(R, HD), v(1024, 8192),
            v(REQ, R, HD), v(REQ, 128, dtype=F32), v(REQ, 128, dtype=F32),
            v(2, 3, 16, R, HD), v(2, 3, 16, 128, dtype=F32),
            v(2, 16, R, HD), v(2, 4, 8, 128, dtype=F32),
            v(2, 3, 4, R, HD), v(2, 3, 8, 128, dtype=F32),
            v(OWN, R, HD), v(2, 8, 128, dtype=F32), v(OWN * R, HD, dtype=F32),
            v(4, R, 1024), v(4, R, 1024), v(3, R, 1024), v(3, R, 1024),
            pltpu.SMEM((SLOTS,), I32), pltpu.SMEM((OWN,), I32), v(8, 128, dtype=I32), pltpu.SMEM((8, 128), I32),
            dma((11,)), dma((2,)), dma((2, 15)), dma((2, 4, 4)),
            dma((2, 3, 2)), dma((2, 3, 2)), dma((2, 3, 2)), dma((2, 3, 2)),
            dma((4,)), dma((4,)), dma((3,)), dma((3,)),
        ],
        name="lent_attention",
        compiler_params=pltpu.CompilerParams(collective_id=0, has_side_effects=True, vmem_limit_bytes=44 * 2**20),
    )(*[pltpu.with_memory_space_constraint(arg, pltpu.HBM) for arg in args])
    return result.reshape(OWN, 4, 1024)


def solution(mesh):
    placed = (
        P("inst", None, "tp", None),
        P("inst", "tp", None, None),
        P("inst", "tp", None, None),
        P("inst", None, "tp", None),
        P("inst", None, "tp", None),
        P("inst"),
        P("inst", "tp", None, None),
        P("inst", "tp", None, None),
        P("inst"),
        P("tp", None),
    )
    return jax.shard_map(
        per_device, mesh=mesh, in_specs=placed, out_specs=P("inst", None, "tp"), check_vma=False
    )
```

```python
import functools

import jax
import jax.numpy as jnp
from jax import lax
from jax.experimental import pallas as pl
from jax.experimental.pallas import tpu as pltpu
from jax.sharding import PartitionSpec as P

MESH = pl.DeviceIdType.MESH
VERY_LOW = -1e30
HD = 128
LOG2E = 1.4426950408889634
SCALE2 = HD**-0.5 * LOG2E
NT = (((1,), (1,)), ((), ()))
F32, BF16, I32 = jnp.float32, jnp.bfloat16, jnp.int32

SLOTS = 48
OWN = 8
REQ = 128
R = 32
GROUPS = (
    ((0, 0), (0, 1), (0, 3), (0, 2)),
    ((2, 0), (3, 0), (1, 0)),
    ((2, 1), (2, 3), (2, 2)),
    ((3, 1), (3, 3), (3, 2)),
    ((1, 1), (1, 3), (1, 2)),
)
GATHER = 30
FORWARD = (2, 3, 1)
FIRST = (2, 1, 3)


def remote(src, dst, send_sem, recv_sem, device):
    return pltpu.make_async_remote_copy(
        src_ref=src, dst_ref=dst, send_sem=send_sem, recv_sem=recv_sem, device_id=device, device_id_type=MESH
    )


def iota(shape, dim):
    return lax.broadcasted_iota(I32, shape, dim)


def to_rows(one_hot, columns):
    copies = jnp.concatenate([columns] * (128 // R), axis=0)
    high = copies.astype(BF16)
    rest = copies - high.astype(F32)
    middle = rest.astype(BF16)
    low = (rest - middle.astype(F32)).astype(BF16)
    parts = [lax.dot_general(one_hot, part, NT, preferred_element_type=F32) for part in (high, middle, low)]
    return parts[0] + parts[1] + parts[2]


def scaled_sums(weights, parts):
    lane, row = iota((R, 128), 1), iota((R, 128), 0)
    diagonal = lane % R == row
    zeros = jnp.zeros((R, 128), BF16)
    picked = [jnp.where(diagonal, jnp.broadcast_to(weights[i : i + 1], (R, 128)), 0.0).astype(BF16) for i in range(4)]
    rows = [jnp.concatenate([zeros, pick] if i % 2 else [pick, zeros], axis=1) for i, pick in enumerate(picked)]
    left = jnp.concatenate(parts[0] + parts[1], axis=0)
    right = jnp.concatenate(parts[2] + parts[3], axis=0)
    result = jnp.dot(jnp.concatenate(rows, axis=0), jnp.concatenate([left, right], axis=1), preferred_element_type=F32)
    return [result[i * R : (i + 1) * R, (i // 2) * 128 : (i // 2 + 1) * 128] for i in range(4)]


def merge_weights(logs):
    top = functools.reduce(jnp.maximum, logs)
    terms = [jnp.exp2(log - top) for log in logs]
    total = functools.reduce(jnp.add, terms)
    inverse = 1.0 / total
    return [term * inverse for term in terms], top + jnp.log2(total)


def by_lane_group(weights):
    group = iota(weights[0].shape, 1) // R
    result = weights[0]
    for k in range(1, len(weights)):
        result = jnp.where(group == k, weights[k], result)
    return result


def kernel(
    sr_hbm, tl_hbm, q_hbm, tk_hbm, tv_hbm, nk_hbm, nv_hbm, pk_hbm, pv_hbm, w_hbm,
    out,
    qall, qown, kb, vb, tkb, tvb, nkb, nvb, wb,
    omsg, lmsg, absent, ro1, rl1, m1, l1, ro2, rl2, lo, lloc, att, cs, cr, ys, yr,
    sr, tl, ivec, inv,
    lsem, qsem, gs, gr, s1, r1, s2, r2, css, crs, yss, yrs,
):
    inst, tp = lax.axis_index("inst"), lax.axis_index("tp")
    z, x, y, c = inst // 4, inst % 4, tp // 2, tp % 2

    def along(half, axis, k):
        if (axis == 0) == (half == 0):
            return {"inst": ((z + k) % 4) * 4 + x}
        return {"inst": z * 4 + (x + k) % 4}

    def place(half):
        return (z, x) if half == 0 else (x, z)

    barrier = pltpu.get_barrier_semaphore()
    peers = [along(0, axis, k) for axis in (0, 1) for k in (2, 1, 3)]
    peers += [{"tp": ((y + k) % 4) * 2 + c} for k in (2, 1, 3)] + [{"tp": y * 2 + 1 - c}]
    for peer in peers:
        pl.semaphore_signal(barrier, inc=1, device_id=peer, device_id_type=MESH)

    def local_copy(i, src, dst):
        copy = pltpu.make_async_copy(src, dst, lsem.at[i])
        copy.start()
        return copy

    c_sr, c_tl = local_copy(9, sr_hbm, sr), local_copy(10, tl_hbm, tl)
    c_qown = local_copy(0, q_hbm, qown)
    c_k, c_v = local_copy(5, pk_hbm, kb), local_copy(6, pv_hbm, vb)
    pl.semaphore_wait(barrier, len(peers))

    sent = []

    def send(src, dst, ss, rs, device):
        copy = remote(src, dst, ss, rs, device)
        copy.start()
        sent.append(copy)

    def all_sent():
        for copy in sent:
            copy.wait_send()
        del sent[:]

    def received(dst, ss, rs):
        remote(dst, dst, ss, rs, along(0, 0, 1)).wait_recv()

    def chunk(half, dp, dq):
        p, q = place(half)
        return pl.ds(half * 64 + (((p + dp) % 4) * 4 + (q + dq) % 4) * 4, 4)

    for axis in (0, 1):
        for k in (2, 1, 3):
            for half in (0, 1):
                back = (4 - k) % 4
                send(
                    q_hbm.at[pl.ds(4 * half, 4)],
                    qall.at[chunk(half, 0, 0)],
                    gs.at[half, axis * 3 + k - 1],
                    gr.at[half, back, 0] if axis == 0 else gr.at[half, 0, back],
                    along(half, axis, k),
                )
    own_copies = []
    for half in (0, 1):
        copy = pltpu.make_async_copy(q_hbm.at[pl.ds(4 * half, 4)], qall.at[chunk(half, 0, 0)], qsem.at[half])
        copy.start()
        own_copies.append(copy)
    c_tk, c_tv = local_copy(1, tk_hbm, tkb), local_copy(2, tv_hbm, tvb)
    c_nk, c_nv = local_copy(3, nk_hbm, nkb), local_copy(4, nv_hbm, nvb)
    c_w = local_copy(7, w_hbm, wb)

    def gathered(half, dp, dq):
        received(qall.at[chunk(half, dp, dq)], gs.at[half, 0], gr.at[half, dp, dq])

    def forward(dp):
        for half in (0, 1):
            gathered(half, dp, 0)
            for k in (2, 1, 3):
                ref = qall.at[chunk(half, dp, 0)]
                send(ref, ref, gs.at[half, 3 + dp * 3 + k - 1], gr.at[half, dp, (4 - k) % 4], along(half, 1, k))

    c_sr.wait()
    c_tl.wait()
    lane8 = iota((8, 128), 1)
    at_slot = jnp.full((8, 128), -1, I32)
    slot_of = jnp.zeros((8, 128), I32)
    for j in range(SLOTS):
        request = sr[j]
        home, half, fourth = request // 8, (request % 8) // 4, request % 4
        swapped = (home % 4) * 4 + home // 4
        position = half * 64 + jnp.where(half == 0, home, swapped) * 4 + fourth
        at_slot = jnp.where(lane8 == j, position, at_slot)
        slot_of = jnp.where(lane8 == position, j, slot_of)
    ivec[...] = slot_of
    c_inv = pltpu.make_async_copy(ivec, inv, lsem.at[8])
    c_inv.start()
    here = (jnp.broadcast_to(at_slot[0:1], (REQ, 128)) == iota((REQ, 128), 0)).astype(F32)
    absent[...] = jnp.broadcast_to((1.0 - jnp.sum(here, axis=1, keepdims=True)) * VERY_LOW, (REQ, 128))
    l1[...] = jnp.zeros_like(l1)
    lloc[...] = jnp.zeros_like(lloc)

    def home_part():
        c_qown.wait()
        c_tk.wait()
        c_tv.wait()
        c_nk.wait()
        c_nv.wait()
        new_scores = lax.dot_general(qown[...].reshape(OWN * R, HD), nkb[...], NT, preferred_element_type=F32)
        token = iota((R, 256), 1)
        new_lane, step = iota((R, 32), 1), iota((R, 32), 0) // 8
        lane, log_columns = iota((R, 128), 1), jnp.zeros((R, 128), F32)
        for r in range(OWN):
            old = lax.dot_general(qown[r], tkb[r], NT, preferred_element_type=F32)
            old = jnp.where(token < tl[r], old, VERY_LOW)
            new = new_scores[r * R : (r + 1) * R]
            new = jnp.where((new_lane >= 4 * r) & (new_lane <= 4 * r + step), new, VERY_LOW)
            peak = jnp.maximum(jnp.max(old, axis=1, keepdims=True), jnp.max(new, axis=1, keepdims=True))
            old = jnp.exp2((old - peak) * SCALE2)
            new = jnp.exp2((new - peak) * SCALE2)
            total = jnp.sum(old, axis=1, keepdims=True) + jnp.sum(new, axis=1, keepdims=True)
            result = jnp.dot(old.astype(BF16), tvb[r], preferred_element_type=F32)
            result = result + jnp.dot(new.astype(BF16), nvb[...], preferred_element_type=F32)
            lo[r] = (result * (1.0 / total)).astype(BF16)
            log_columns = jnp.where(lane == r, peak * SCALE2 + jnp.log2(total), log_columns)
        pick = (iota((OWN, 128), 0) == iota((OWN, 128), 1)).astype(F32).astype(BF16)
        rows = to_rows(pick, log_columns)
        lloc[0, 0:4] = rows[0:4]
        lloc[1, 0:4] = rows[4:8]

    def lend(chunks):
        lane, zeros = iota((R, 128), 1), jnp.zeros((R, HD), BF16)
        todo = []
        for half, dp, dq in chunks:
            p, q = place(half)
            line, column = (p + dp) % 4, ((q + dq) % 4) * 4
            base = pl.multiple_of(half * 64 + line * 16 + column, 4)
            todo += [((half, dp), base + i, column + i) for i in (0, 2)]
        log_columns = {}
        for half, dp, _ in chunks:
            if (half, dp) not in log_columns:
                log_columns[half, dp] = logs_of[half, dp]
        slots = [[inv[0, first + u] for u in (0, 1)] for _, first, _ in todo]
        scores = []
        for (_, first, _), (a, b) in zip(todo, slots):
            queries = [qall[first + u] for u in (0, 1)]
            queries = [jnp.concatenate([queries[0], zeros], axis=1), jnp.concatenate([zeros, queries[1]], axis=1)]
            keys = jnp.concatenate([kb[a], kb[b]], axis=1)
            scores.append(lax.dot_general(jnp.concatenate(queries, axis=0), keys, NT, preferred_element_type=F32))
        peaks = [jnp.max(score, axis=1, keepdims=True) for score in scores]
        terms = [jnp.exp2((score - peak) * SCALE2) for score, peak in zip(scores, peaks)]
        totals = [jnp.sum(term, axis=1, keepdims=True) for term in terms]
        for (key, first, column), (a, b), peak, term, total in zip(todo, slots, peaks, terms, totals):
            values = jnp.concatenate([vb[a], vb[b]], axis=1)
            result = jnp.dot(term.astype(BF16), values, preferred_element_type=F32)
            inverse = 1.0 / total
            logs = peak * SCALE2 + jnp.log2(total)
            omsg[first] = (result[:R, :HD] * inverse[:R]).astype(BF16)
            omsg[first + 1] = (result[R:, HD:] * inverse[R:]).astype(BF16)
            log_columns[key] = jnp.where(lane == column, logs[:R], log_columns[key])
            log_columns[key] = jnp.where(lane == column + 1, logs[R:], log_columns[key])
        for key in log_columns:
            logs_of[key] = log_columns[key]

    def send_line(dp):
        pick = (iota((16, 128), 0) == iota((16, 128), 1)).astype(F32).astype(BF16)
        parts = []
        for half in (0, 1):
            p, _ = place(half)
            parts.append(pl.ds(pl.multiple_of(half * 64 + ((p + dp) % 4) * 16, 16), 16))
            if dp:
                send(omsg.at[parts[half]], ro1.at[half, dp - 1], s1.at[half, dp - 1, 0], r1.at[half, dp - 1, 0], along(half, 0, dp))
        for half, part in enumerate(parts):
            lmsg[part] = to_rows(pick, logs_of[half, dp]) + absent[part]
            if dp:
                send(lmsg.at[part], rl1.at[half, dp - 1], s1.at[half, dp - 1, 1], r1.at[half, dp - 1, 1], along(half, 0, dp))

    def first_merge(half):
        p, q = place(half)
        base = pl.multiple_of(half * 64 + p * 16, 16)
        for k in FIRST:
            received(rl1.at[half, k - 1], s1.at[half, 0, 0], r1.at[half, k - 1, 1])
        weights, log = merge_weights([lmsg[pl.ds(base, 16)]] + [rl1[half, k] for k in range(3)])
        weights = by_lane_group(weights)
        for i in range(4):
            l1[half, i, 0:4] = log[4 * i : 4 * i + 4]
        for k in FIRST:
            received(ro1.at[half, k - 1], s1.at[half, 0, 0], r1.at[half, k - 1, 0])
        for i in range(0, 16, 4):
            parts = [[omsg[base + i + u]] + [ro1[half, k, i + u] for k in range(3)] for u in range(4)]
            for u, result in enumerate(scaled_sums(weights[i : i + 4], parts)):
                m1[half, i + u] = result.astype(BF16)
        for k in (2, 1, 3):
            other = (q + k) % 4
            to = along(half, 1, k)
            send(m1.at[half, pl.ds(other * 4, 4)], ro2.at[half, k - 1], s2.at[half, k - 1, 1], r2.at[half, k - 1, 1], to)
            send(l1.at[half, other], rl2.at[half, k - 1], s2.at[half, k - 1, 0], r2.at[half, k - 1, 0], to)

    def second_merge(half):
        _, q = place(half)
        for k in (1, 3, 2):
            received(rl2.at[half, k - 1], s2.at[half, 0, 0], r2.at[half, k - 1, 0])
        weights, _ = merge_weights([l1[half, q]] + [rl2[half, k] for k in range(3)] + [lloc[half]])
        lent, home = by_lane_group(weights[:4]), weights[4]
        lane, row = iota((R, 128), 1), iota((R, 128), 0)
        picked = [
            jnp.where(lane == row + u * R, jnp.broadcast_to(home[u : u + 1], (R, 128)), 0.0).astype(BF16) for u in range(4)
        ]
        homes = jnp.concatenate([lo[half * 4 + u] for u in range(4)], axis=0)
        own = jnp.dot(jnp.concatenate(picked, axis=0), homes, preferred_element_type=F32)
        for k in (1, 3, 2):
            received(ro2.at[half, k - 1], s2.at[half, 0, 0], r2.at[half, k - 1, 1])
        parts = [[m1[half, q * 4 + u]] + [ro2[half, k, u] for k in range(3)] for u in range(4)]
        for u, result in enumerate(scaled_sums(lent[0:4], parts)):
            att[(half * 4 + u) * R : (half * 4 + u + 1) * R] = result + own[u * R : (u + 1) * R]

    home_part()
    for dp in FORWARD:
        forward(dp)
    c_inv.wait()
    for copy in own_copies:
        copy.wait()
    logs_of = {(half, dp): jnp.zeros((R, 128), F32) for half in (0, 1) for dp in range(4)}
    c_k.wait()
    c_v.wait()
    seen = {0: 0, 1: 0, 2: 0, 3: 0}
    for pairs in GROUPS:
        chunks = [(half, dp, dq) for dp, dq in pairs for half in (0, 1)]
        for half, dp, dq in chunks:
            if dq:
                gathered(half, dp, dq)
        lend(chunks)
        for dp, dq in pairs:
            seen[dp] += 1
        for dp in sorted({dp for dp, _ in pairs if seen[dp] == 4}):
            send_line(dp)
    lent = sent[GATHER:]
    del sent[GATHER:]
    all_sent()
    for half in (0, 1):
        first_merge(half)
    for copy in lent:
        copy.wait_send()
    for half in (0, 1):
        second_merge(half)

    flat = jnp.concatenate([att[pl.ds(h, R, stride=8)].astype(BF16) for h in range(8)], axis=1)
    c_w.wait()

    def columns(target):
        return jnp.dot(flat, wb[:, pl.ds(pl.multiple_of(target * 1024, 1024), 1024)], preferred_element_type=F32)

    def share(dy):
        cs[dy] = columns(((y + dy) % 4) * 2 + 1 - c).astype(BF16)
        send(cs.at[dy], cr.at[dy], css.at[dy], crs.at[dy], {"tp": y * 2 + 1 - c})

    def both(dy):
        value = columns(((y + dy) % 4) * 2 + c)
        received(cr.at[dy], css.at[dy], crs.at[dy])
        return value + cr[dy].astype(F32)

    def along_y(dy):
        ys[dy - 1] = both(dy).astype(BF16)
        send(ys.at[dy - 1], yr.at[dy - 1], yss.at[dy - 1], yrs.at[dy - 1], {"tp": ((y + dy) % 4) * 2 + c})

    share(2)
    share(1)
    share(3)
    along_y(2)
    along_y(1)
    along_y(3)
    share(0)
    value = both(0)
    last = sent[-4:]
    del sent[-4:]
    all_sent()
    for dy in (2, 1, 3):
        received(yr.at[dy - 1], yss.at[dy - 1], yrs.at[dy - 1])
        value = value + yr[dy - 1].astype(F32)
    out[...] = value.astype(BF16)
    for copy in last:
        copy.wait_send()


def per_device(
    queries, tail_keys, tail_values, new_keys, new_values, tail_lengths, pool_keys, pool_values, slot_request, out_weight
):
    in_hbm = pl.BlockSpec(memory_space=pltpu.HBM)
    dma = pltpu.SemaphoreType.DMA

    def v(*shape, dtype=BF16):
        return pltpu.VMEM(shape, dtype)

    args = (
        slot_request,
        tail_lengths,
        queries.reshape(OWN, R, HD),
        tail_keys.reshape(OWN, 256, HD),
        tail_values.reshape(OWN, 256, HD),
        new_keys.reshape(R, HD),
        new_values.reshape(R, HD),
        pool_keys.reshape(SLOTS, 256, HD),
        pool_values.reshape(SLOTS, 256, HD),
        out_weight,
    )
    result = pl.pallas_call(
        kernel,
        out_shape=jax.ShapeDtypeStruct((R, 1024), BF16),
        in_specs=[in_hbm] * len(args),
        out_specs=pl.BlockSpec(memory_space=pltpu.VMEM),
        scratch_shapes=[
            v(REQ, R, HD), v(OWN, R, HD), v(SLOTS, 256, HD), v(SLOTS, 256, HD), v(OWN, 256, HD), v(OWN, 256, HD),
            v(R, HD), v(R, HD), v(1024, 8192),
            v(REQ, R, HD), v(REQ, 128, dtype=F32), v(REQ, 128, dtype=F32),
            v(2, 3, 16, R, HD), v(2, 3, 16, 128, dtype=F32),
            v(2, 16, R, HD), v(2, 4, 8, 128, dtype=F32),
            v(2, 3, 4, R, HD), v(2, 3, 8, 128, dtype=F32),
            v(OWN, R, HD), v(2, 8, 128, dtype=F32), v(OWN * R, HD, dtype=F32),
            v(4, R, 1024), v(4, R, 1024), v(3, R, 1024), v(3, R, 1024),
            pltpu.SMEM((SLOTS,), I32), pltpu.SMEM((OWN,), I32), v(8, 128, dtype=I32), pltpu.SMEM((8, 128), I32),
            dma((11,)), dma((2,)), dma((2, 15)), dma((2, 4, 4)),
            dma((2, 3, 2)), dma((2, 3, 2)), dma((2, 3, 2)), dma((2, 3, 2)),
            dma((4,)), dma((4,)), dma((3,)), dma((3,)),
        ],
        name="lent_attention",
        compiler_params=pltpu.CompilerParams(collective_id=0, has_side_effects=True, vmem_limit_bytes=44 * 2**20),
    )(*[pltpu.with_memory_space_constraint(arg, pltpu.HBM) for arg in args])
    return result.reshape(OWN, 4, 1024)


def solution(mesh):
    placed = (
        P("inst", None, "tp", None),
        P("inst", "tp", None, None),
        P("inst", "tp", None, None),
        P("inst", None, "tp", None),
        P("inst", None, "tp", None),
        P("inst"),
        P("inst", "tp", None, None),
        P("inst", "tp", None, None),
        P("inst"),
        P("tp", None),
    )
    return jax.shard_map(
        per_device, mesh=mesh, in_specs=placed, out_specs=P("inst", None, "tp"), check_vma=False
    )
```

```python
import functools

import jax
import jax.numpy as jnp
from jax import lax
from jax.experimental import pallas as pl
from jax.experimental.pallas import tpu as pltpu
from jax.sharding import PartitionSpec as P

MESH = pl.DeviceIdType.MESH
VERY_LOW = -1e30
HD = 128
LOG2E = 1.4426950408889634
SCALE2 = HD**-0.5 * LOG2E
NT = (((1,), (1,)), ((), ()))
F32, BF16, I32 = jnp.float32, jnp.bfloat16, jnp.int32

SLOTS = 48
OWN = 8
REQ = 128
R = 32
GROUPS = (
    ((0, 0), (0, 1), (0, 3), (0, 2)),
    ((2, 0), (3, 0), (1, 0)),
    ((2, 1), (2, 3), (2, 2)),
    ((3, 1), (3, 3), (3, 2)),
    ((1, 1), (1, 3), (1, 2)),
)
EARLY = 4
GATHER = 30
FORWARD = (2, 3, 1)
FIRST = (2, 1, 3)


def remote(src, dst, send_sem, recv_sem, device):
    return pltpu.make_async_remote_copy(
        src_ref=src, dst_ref=dst, send_sem=send_sem, recv_sem=recv_sem, device_id=device, device_id_type=MESH
    )


def iota(shape, dim):
    return lax.broadcasted_iota(I32, shape, dim)


def to_rows(one_hot, columns):
    copies = jnp.concatenate([columns] * (128 // R), axis=0)
    high = copies.astype(BF16)
    rest = copies - high.astype(F32)
    middle = rest.astype(BF16)
    low = (rest - middle.astype(F32)).astype(BF16)
    parts = [lax.dot_general(one_hot, part, NT, preferred_element_type=F32) for part in (high, middle, low)]
    return parts[0] + parts[1] + parts[2]


def scaled_sums(weights, parts):
    lane, row = iota((R, 128), 1), iota((R, 128), 0)
    diagonal = lane % R == row
    zeros = jnp.zeros((R, 128), BF16)
    picked = [jnp.where(diagonal, jnp.broadcast_to(weights[i : i + 1], (R, 128)), 0.0).astype(BF16) for i in range(4)]
    rows = [jnp.concatenate([zeros, pick] if i % 2 else [pick, zeros], axis=1) for i, pick in enumerate(picked)]
    left = jnp.concatenate(parts[0] + parts[1], axis=0)
    right = jnp.concatenate(parts[2] + parts[3], axis=0)
    result = jnp.dot(jnp.concatenate(rows, axis=0), jnp.concatenate([left, right], axis=1), preferred_element_type=F32)
    return [result[i * R : (i + 1) * R, (i // 2) * 128 : (i // 2 + 1) * 128] for i in range(4)]


def merge_weights(logs):
    top = functools.reduce(jnp.maximum, logs)
    terms = [jnp.exp2(log - top) for log in logs]
    total = functools.reduce(jnp.add, terms)
    inverse = 1.0 / total
    return [term * inverse for term in terms], top + jnp.log2(total)


def by_lane_group(weights):
    group = iota(weights[0].shape, 1) // R
    result = weights[0]
    for k in range(1, len(weights)):
        result = jnp.where(group == k, weights[k], result)
    return result


def kernel(
    sr_hbm, tl_hbm, q_hbm, tk_hbm, tv_hbm, nk_hbm, nv_hbm, pk_hbm, pv_hbm, w_hbm,
    out,
    qall, qown, kb, vb, tkb, tvb, nkb, nvb, wb,
    omsg, lmsg, absent, ro1, rl1, m1, l1, ro2, rl2, lo, lloc, att, cs, cr, ys, yr,
    sr, tl, ivec, inv,
    lsem, qsem, gs, gr, s1, r1, s2, r2, css, crs, yss, yrs,
):
    inst, tp = lax.axis_index("inst"), lax.axis_index("tp")
    z, x, y, c = inst // 4, inst % 4, tp // 2, tp % 2

    def along(half, axis, k):
        if (axis == 0) == (half == 0):
            return {"inst": ((z + k) % 4) * 4 + x}
        return {"inst": z * 4 + (x + k) % 4}

    barrier = pltpu.get_barrier_semaphore()
    peers = [along(0, axis, k) for axis in (0, 1) for k in (2, 1, 3)]
    peers += [{"tp": ((y + k) % 4) * 2 + c} for k in (2, 1, 3)] + [{"tp": y * 2 + 1 - c}]
    for peer in peers:
        pl.semaphore_signal(barrier, inc=1, device_id=peer, device_id_type=MESH)

    def local_copy(i, src, dst):
        copy = pltpu.make_async_copy(src, dst, lsem.at[i])
        copy.start()
        return copy

    c_sr, c_tl = local_copy(9, sr_hbm, sr), local_copy(10, tl_hbm, tl)
    c_qown = local_copy(0, q_hbm, qown)
    c_k, c_v = local_copy(5, pk_hbm, kb), local_copy(6, pv_hbm, vb)
    pl.semaphore_wait(barrier, len(peers))

    sent = []

    def send(src, dst, ss, rs, device):
        copy = remote(src, dst, ss, rs, device)
        copy.start()
        sent.append(copy)

    def all_sent():
        for copy in sent:
            copy.wait_send()
        del sent[:]

    def received(dst, ss, rs):
        remote(dst, dst, ss, rs, along(0, 0, 1)).wait_recv()

    def chunk(half, dp, dq):
        return pl.ds(half * 64 + dp * 16 + dq * 4, 4)

    c_qown.wait()
    for axis in (0, 1):
        for k in (2, 1, 3):
            for half in (0, 1):
                back = (4 - k) % 4
                send(
                    qown.at[pl.ds(4 * half, 4)],
                    qall.at[chunk(half, back, 0) if axis == 0 else chunk(half, 0, back)],
                    gs.at[half, axis * 3 + k - 1],
                    gr.at[half, back, 0] if axis == 0 else gr.at[half, 0, back],
                    along(half, axis, k),
                )
    own_copies = []
    for half in (0, 1):
        copy = pltpu.make_async_copy(qown.at[pl.ds(4 * half, 4)], qall.at[chunk(half, 0, 0)], qsem.at[half])
        copy.start()
        own_copies.append(copy)
    c_tk, c_tv = local_copy(1, tk_hbm, tkb), local_copy(2, tv_hbm, tvb)
    c_nk, c_nv = local_copy(3, nk_hbm, nkb), local_copy(4, nv_hbm, nvb)
    c_w = local_copy(7, w_hbm, wb)

    def gathered(half, dp, dq):
        received(qall.at[chunk(half, dp, dq)], gs.at[half, 0], gr.at[half, dp, dq])

    def forward(dp):
        for half in (0, 1):
            gathered(half, dp, 0)
            for k in (2, 1, 3):
                to = qall.at[chunk(half, dp, (4 - k) % 4)]
                send(qall.at[chunk(half, dp, 0)], to, gs.at[half, 3 + dp * 3 + k - 1], gr.at[half, dp, (4 - k) % 4], along(half, 1, k))

    c_sr.wait()
    c_tl.wait()
    lane8 = iota((8, 128), 1)
    at_slot = jnp.full((8, 128), -1, I32)
    slot_of = jnp.zeros((8, 128), I32)
    for j in range(SLOTS):
        request = sr[j]
        home, half, fourth = request // 8, (request % 8) // 4, request % 4
        dz, dx = (home // 4 - z + 4) % 4, (home % 4 - x + 4) % 4
        position = half * 64 + jnp.where(half == 0, dz * 4 + dx, dx * 4 + dz) * 4 + fourth
        at_slot = jnp.where(lane8 == j, position, at_slot)
        slot_of = jnp.where(lane8 == position, j, slot_of)
    ivec[...] = slot_of
    c_inv = pltpu.make_async_copy(ivec, inv, lsem.at[8])
    c_inv.start()
    here = (jnp.broadcast_to(at_slot[0:1], (REQ, 128)) == iota((REQ, 128), 0)).astype(F32)
    absent[...] = jnp.broadcast_to((1.0 - jnp.sum(here, axis=1, keepdims=True)) * VERY_LOW, (REQ, 128))
    l1[...] = jnp.zeros_like(l1)
    lloc[...] = jnp.zeros_like(lloc)

    def home_part():
        c_tk.wait()
        c_tv.wait()
        c_nk.wait()
        c_nv.wait()
        new_scores = lax.dot_general(qown[...].reshape(OWN * R, HD), nkb[...], NT, preferred_element_type=F32)
        token = iota((R, 256), 1)
        new_lane, step = iota((R, 32), 1), iota((R, 32), 0) // 8
        lane, log_columns = iota((R, 128), 1), jnp.zeros((R, 128), F32)
        for r in range(OWN):
            old = lax.dot_general(qown[r], tkb[r], NT, preferred_element_type=F32)
            old = jnp.where(token < tl[r], old, VERY_LOW)
            new = new_scores[r * R : (r + 1) * R]
            new = jnp.where((new_lane >= 4 * r) & (new_lane <= 4 * r + step), new, VERY_LOW)
            peak = jnp.maximum(jnp.max(old, axis=1, keepdims=True), jnp.max(new, axis=1, keepdims=True))
            old = jnp.exp2((old - peak) * SCALE2)
            new = jnp.exp2((new - peak) * SCALE2)
            total = jnp.sum(old, axis=1, keepdims=True) + jnp.sum(new, axis=1, keepdims=True)
            result = jnp.dot(old.astype(BF16), tvb[r], preferred_element_type=F32)
            result = result + jnp.dot(new.astype(BF16), nvb[...], preferred_element_type=F32)
            lo[r] = (result * (1.0 / total)).astype(BF16)
            log_columns = jnp.where(lane == r, peak * SCALE2 + jnp.log2(total), log_columns)
        pick = (iota((OWN, 128), 0) == iota((OWN, 128), 1)).astype(F32).astype(BF16)
        rows = to_rows(pick, log_columns)
        lloc[0, 0:4] = rows[0:4]
        lloc[1, 0:4] = rows[4:8]

    def lend(chunks):
        lane, zeros = iota((R, 128), 1), jnp.zeros((R, HD), BF16)
        todo = []
        for half, dp, dq in chunks:
            todo += [((half, dp), half * 64 + dp * 16 + dq * 4 + i, dq * 4 + i) for i in (0, 2)]
        log_columns = {}
        for half, dp, _ in chunks:
            if (half, dp) not in log_columns:
                log_columns[half, dp] = logs_of[half, dp]
        slots = [[inv[0, first + u] for u in (0, 1)] for _, first, _ in todo]
        scores = []
        for (_, first, _), (a, b) in zip(todo, slots):
            queries = [qall[first + u] for u in (0, 1)]
            queries = [jnp.concatenate([queries[0], zeros], axis=1), jnp.concatenate([zeros, queries[1]], axis=1)]
            keys = jnp.concatenate([kb[a], kb[b]], axis=1)
            scores.append(lax.dot_general(jnp.concatenate(queries, axis=0), keys, NT, preferred_element_type=F32))
        peaks = [jnp.max(score, axis=1, keepdims=True) for score in scores]
        terms = [jnp.exp2((score - peak) * SCALE2) for score, peak in zip(scores, peaks)]
        totals = [jnp.sum(term, axis=1, keepdims=True) for term in terms]
        for (key, first, column), (a, b), peak, term, total in zip(todo, slots, peaks, terms, totals):
            values = jnp.concatenate([vb[a], vb[b]], axis=1)
            result = jnp.dot(term.astype(BF16), values, preferred_element_type=F32)
            inverse = 1.0 / total
            logs = peak * SCALE2 + jnp.log2(total)
            omsg[first] = (result[:R, :HD] * inverse[:R]).astype(BF16)
            omsg[first + 1] = (result[R:, HD:] * inverse[R:]).astype(BF16)
            log_columns[key] = jnp.where(lane == column, logs[:R], log_columns[key])
            log_columns[key] = jnp.where(lane == column + 1, logs[R:], log_columns[key])
        for key in log_columns:
            logs_of[key] = log_columns[key]

    def send_line(dp):
        pick = (iota((16, 128), 0) == iota((16, 128), 1)).astype(F32).astype(BF16)
        for half in (0, 1):
            send_part(half, dp, EARLY if dp in (1, 3) else 0, 16)
        for half in (0, 1):
            part = pl.ds(half * 64 + dp * 16, 16)
            lmsg[part] = to_rows(pick, logs_of[half, dp]) + absent[part]
            if dp:
                send(lmsg.at[part], rl1.at[half, dp - 1], s1.at[half, dp - 1, 2], r1.at[half, dp - 1, 2], along(half, 0, dp))
        if dp == 2 and EARLY:
            for half in (0, 1):
                for other in (3, 1):
                    send_part(half, other, 0, EARLY)

    def send_part(half, dp, start, end):
        if dp:
            send(
                omsg.at[pl.ds(half * 64 + dp * 16 + start, end - start)],
                ro1.at[half, dp - 1, pl.ds(start, end - start)],
                s1.at[half, dp - 1, int(start > 0)],
                r1.at[half, dp - 1, int(start > 0)],
                along(half, 0, dp),
            )

    def first_merge(half):
        base = half * 64
        for k in FIRST:
            received(rl1.at[half, k - 1], s1.at[half, 0, 0], r1.at[half, k - 1, 2])
        weights, log = merge_weights([lmsg[pl.ds(base, 16)]] + [rl1[half, k] for k in range(3)])
        weights = by_lane_group(weights)
        for i in range(4):
            l1[half, i, 0:4] = log[4 * i : 4 * i + 4]
        for k in FIRST:
            for start, end in ((0, EARLY), (EARLY, 16)) if EARLY and k != 2 else ((0, 16),):
                received(ro1.at[half, k - 1, pl.ds(start, end - start)], s1.at[half, 0, 0], r1.at[half, k - 1, int(start > 0)])
        for i in range(0, 16, 4):
            parts = [[omsg[base + i + u]] + [ro1[half, k, i + u] for k in range(3)] for u in range(4)]
            for u, result in enumerate(scaled_sums(weights[i : i + 4], parts)):
                m1[half, i + u] = result.astype(BF16)
        for k in (2, 1, 3):
            to = along(half, 1, k)
            send(m1.at[half, pl.ds(k * 4, 4)], ro2.at[half, k - 1], s2.at[half, k - 1, 1], r2.at[half, k - 1, 1], to)
            send(l1.at[half, k], rl2.at[half, k - 1], s2.at[half, k - 1, 0], r2.at[half, k - 1, 0], to)

    def second_merge(half):
        for k in (1, 3, 2):
            received(rl2.at[half, k - 1], s2.at[half, 0, 0], r2.at[half, k - 1, 0])
        weights, _ = merge_weights([l1[half, 0]] + [rl2[half, k] for k in range(3)] + [lloc[half]])
        lent, home = by_lane_group(weights[:4]), weights[4]
        lane, row = iota((R, 128), 1), iota((R, 128), 0)
        picked = [
            jnp.where(lane == row + u * R, jnp.broadcast_to(home[u : u + 1], (R, 128)), 0.0).astype(BF16) for u in range(4)
        ]
        homes = jnp.concatenate([lo[half * 4 + u] for u in range(4)], axis=0)
        own = jnp.dot(jnp.concatenate(picked, axis=0), homes, preferred_element_type=F32)
        for k in (1, 3, 2):
            received(ro2.at[half, k - 1], s2.at[half, 0, 0], r2.at[half, k - 1, 1])
        parts = [[m1[half, u]] + [ro2[half, k, u] for k in range(3)] for u in range(4)]
        for u, result in enumerate(scaled_sums(lent[0:4], parts)):
            att[(half * 4 + u) * R : (half * 4 + u + 1) * R] = result + own[u * R : (u + 1) * R]

    for dp in FORWARD:
        forward(dp)
    c_inv.wait()
    for copy in own_copies:
        copy.wait()
    logs_of = {(half, dp): jnp.zeros((R, 128), F32) for half in (0, 1) for dp in range(4)}
    c_k.wait()
    c_v.wait()
    seen = {0: 0, 1: 0, 2: 0, 3: 0}
    for pairs in GROUPS:
        chunks = [(half, dp, dq) for dp, dq in pairs for half in (0, 1)]
        for half, dp, dq in chunks:
            if dq:
                gathered(half, dp, dq)
        lend(chunks)
        for dp, dq in pairs:
            seen[dp] += 1
        for dp in sorted({dp for dp, _ in pairs if seen[dp] == 4}):
            send_line(dp)
    home_part()
    lent = sent[GATHER:]
    del sent[GATHER:]
    all_sent()
    for half in (0, 1):
        first_merge(half)
    for copy in lent:
        copy.wait_send()
    for half in (0, 1):
        second_merge(half)

    flat = jnp.concatenate([att[pl.ds(h, R, stride=8)].astype(BF16) for h in range(8)], axis=1)
    c_w.wait()

    def columns(target):
        return jnp.dot(flat, wb[:, pl.ds(pl.multiple_of(target * 1024, 1024), 1024)], preferred_element_type=F32)

    def share(dy):
        cs[dy] = columns(((y + dy) % 4) * 2 + 1 - c).astype(BF16)
        send(cs.at[dy], cr.at[dy], css.at[dy], crs.at[dy], {"tp": y * 2 + 1 - c})

    def both(dy):
        value = columns(((y + dy) % 4) * 2 + c)
        received(cr.at[dy], css.at[dy], crs.at[dy])
        return value + cr[dy].astype(F32)

    def along_y(dy):
        ys[dy - 1] = both(dy).astype(BF16)
        send(ys.at[dy - 1], yr.at[dy - 1], yss.at[dy - 1], yrs.at[dy - 1], {"tp": ((y + dy) % 4) * 2 + c})

    share(2)
    share(1)
    share(3)
    along_y(2)
    along_y(1)
    along_y(3)
    share(0)
    value = both(0)
    last = sent[-4:]
    del sent[-4:]
    all_sent()
    for dy in (2, 1, 3):
        received(yr.at[dy - 1], yss.at[dy - 1], yrs.at[dy - 1])
        value = value + yr[dy - 1].astype(F32)
    out[...] = value.astype(BF16)
    for copy in last:
        copy.wait_send()


def per_device(
    queries, tail_keys, tail_values, new_keys, new_values, tail_lengths, pool_keys, pool_values, slot_request, out_weight
):
    in_hbm = pl.BlockSpec(memory_space=pltpu.HBM)
    dma = pltpu.SemaphoreType.DMA

    def v(*shape, dtype=BF16):
        return pltpu.VMEM(shape, dtype)

    args = (
        slot_request,
        tail_lengths,
        queries.reshape(OWN, R, HD),
        tail_keys.reshape(OWN, 256, HD),
        tail_values.reshape(OWN, 256, HD),
        new_keys.reshape(R, HD),
        new_values.reshape(R, HD),
        pool_keys.reshape(SLOTS, 256, HD),
        pool_values.reshape(SLOTS, 256, HD),
        out_weight,
    )
    result = pl.pallas_call(
        kernel,
        out_shape=jax.ShapeDtypeStruct((R, 1024), BF16),
        in_specs=[in_hbm] * len(args),
        out_specs=pl.BlockSpec(memory_space=pltpu.VMEM),
        scratch_shapes=[
            v(REQ, R, HD), v(OWN, R, HD), v(SLOTS, 256, HD), v(SLOTS, 256, HD), v(OWN, 256, HD), v(OWN, 256, HD),
            v(R, HD), v(R, HD), v(1024, 8192),
            v(REQ, R, HD), v(REQ, 128, dtype=F32), v(REQ, 128, dtype=F32),
            v(2, 3, 16, R, HD), v(2, 3, 16, 128, dtype=F32),
            v(2, 16, R, HD), v(2, 4, 8, 128, dtype=F32),
            v(2, 3, 4, R, HD), v(2, 3, 8, 128, dtype=F32),
            v(OWN, R, HD), v(2, 8, 128, dtype=F32), v(OWN * R, HD, dtype=F32),
            v(4, R, 1024), v(4, R, 1024), v(3, R, 1024), v(3, R, 1024),
            pltpu.SMEM((SLOTS,), I32), pltpu.SMEM((OWN,), I32), v(8, 128, dtype=I32), pltpu.SMEM((8, 128), I32),
            dma((11,)), dma((2,)), dma((2, 15)), dma((2, 4, 4)),
            dma((2, 3, 3)), dma((2, 3, 3)), dma((2, 3, 2)), dma((2, 3, 2)),
            dma((4,)), dma((4,)), dma((3,)), dma((3,)),
        ],
        name="lent_attention",
        compiler_params=pltpu.CompilerParams(collective_id=0, has_side_effects=True, vmem_limit_bytes=44 * 2**20),
    )(*[pltpu.with_memory_space_constraint(arg, pltpu.HBM) for arg in args])
    return result.reshape(OWN, 4, 1024)


def solution(mesh):
    placed = (
        P("inst", None, "tp", None),
        P("inst", "tp", None, None),
        P("inst", "tp", None, None),
        P("inst", None, "tp", None),
        P("inst", None, "tp", None),
        P("inst"),
        P("inst", "tp", None, None),
        P("inst", "tp", None, None),
        P("inst"),
        P("tp", None),
    )
    return jax.shard_map(
        per_device, mesh=mesh, in_specs=placed, out_specs=P("inst", None, "tp"), check_vma=False
    )
```

```python
import functools

import jax
import jax.numpy as jnp
from jax import lax
from jax.experimental import pallas as pl
from jax.experimental.pallas import tpu as pltpu
from jax.sharding import PartitionSpec as P

MESH = pl.DeviceIdType.MESH
VERY_LOW = -1e30
HD = 128
LOG2E = 1.4426950408889634
SCALE2 = HD**-0.5 * LOG2E
NT = (((1,), (1,)), ((), ()))
F32, BF16, I32 = jnp.float32, jnp.bfloat16, jnp.int32

SLOTS = 48
OWN = 8
REQ = 128
R = 32
GROUPS = (
    ((0, 0), (0, 1), (0, 3), (0, 2)),
    ((2, 0), (3, 0), (1, 0)),
    ((2, 1), (2, 3), (2, 2)),
    ((3, 1), (3, 3), (3, 2)),
    ((1, 1), (1, 3), (1, 2)),
)
EARLY = 4
GATHER = 30
FORWARD = (2, 3, 1)
FIRST = (2, 1, 3)


def remote(src, dst, send_sem, recv_sem, device):
    return pltpu.make_async_remote_copy(
        src_ref=src, dst_ref=dst, send_sem=send_sem, recv_sem=recv_sem, device_id=device, device_id_type=MESH
    )


def iota(shape, dim):
    return lax.broadcasted_iota(I32, shape, dim)


def to_rows(one_hot, columns):
    copies = jnp.concatenate([columns] * (128 // R), axis=0)
    high = copies.astype(BF16)
    rest = copies - high.astype(F32)
    middle = rest.astype(BF16)
    low = (rest - middle.astype(F32)).astype(BF16)
    parts = [lax.dot_general(one_hot, part, NT, preferred_element_type=F32) for part in (high, middle, low)]
    return parts[0] + parts[1] + parts[2]


def scaled_sums(weights, parts):
    lane, row = iota((R, 128), 1), iota((R, 128), 0)
    diagonal = lane % R == row
    zeros = jnp.zeros((R, 128), BF16)
    picked = [jnp.where(diagonal, jnp.broadcast_to(weights[i : i + 1], (R, 128)), 0.0).astype(BF16) for i in range(4)]
    rows = [jnp.concatenate([zeros, pick] if i % 2 else [pick, zeros], axis=1) for i, pick in enumerate(picked)]
    left = jnp.concatenate(parts[0] + parts[1], axis=0)
    right = jnp.concatenate(parts[2] + parts[3], axis=0)
    result = jnp.dot(jnp.concatenate(rows, axis=0), jnp.concatenate([left, right], axis=1), preferred_element_type=F32)
    return [result[i * R : (i + 1) * R, (i // 2) * 128 : (i // 2 + 1) * 128] for i in range(4)]


def merge_weights(logs):
    top = functools.reduce(jnp.maximum, logs)
    terms = [jnp.exp2(log - top) for log in logs]
    total = functools.reduce(jnp.add, terms)
    inverse = 1.0 / total
    return [term * inverse for term in terms], top + jnp.log2(total)


def by_lane_group(weights):
    group = iota(weights[0].shape, 1) // R
    result = weights[0]
    for k in range(1, len(weights)):
        result = jnp.where(group == k, weights[k], result)
    return result


def kernel(
    sr_hbm, tl_hbm, q_hbm, tk_hbm, tv_hbm, nk_hbm, nv_hbm, pk_hbm, pv_hbm, w_hbm,
    out,
    qall, qown, kb, vb, tkb, tvb, nkb, nvb, wb,
    omsg, lmsg, absent, ro1, rl1, m1, l1, ro2, rl2, lo, lloc, att, cs, cr, ys, yr,
    sr, tl, ivec, inv,
    lsem, qsem, gs, gr, s1, r1, s2, r2, css, crs, yss, yrs,
):
    inst, tp = lax.axis_index("inst"), lax.axis_index("tp")
    z, x, y, c = inst // 4, inst % 4, tp // 2, tp % 2

    def along(half, axis, k):
        if (axis == 0) == (half == 0):
            return {"inst": ((z + k) % 4) * 4 + x}
        return {"inst": z * 4 + (x + k) % 4}

    barrier = pltpu.get_barrier_semaphore()
    peers = [along(0, axis, k) for axis in (0, 1) for k in (2, 1, 3)]
    peers += [{"tp": ((y + k) % 4) * 2 + c} for k in (2, 1, 3)] + [{"tp": y * 2 + 1 - c}]
    for peer in peers:
        pl.semaphore_signal(barrier, inc=1, device_id=peer, device_id_type=MESH)

    def local_copy(i, src, dst):
        copy = pltpu.make_async_copy(src, dst, lsem.at[i])
        copy.start()
        return copy

    c_sr, c_tl = local_copy(9, sr_hbm, sr), local_copy(10, tl_hbm, tl)
    c_qown = local_copy(0, q_hbm, qown)
    c_k, c_v = local_copy(5, pk_hbm, kb), local_copy(6, pv_hbm, vb)
    pl.semaphore_wait(barrier, len(peers))

    sent = []

    def send(src, dst, ss, rs, device):
        copy = remote(src, dst, ss, rs, device)
        copy.start()
        sent.append(copy)

    def all_sent():
        for copy in sent:
            copy.wait_send()
        del sent[:]

    def received(dst, ss, rs):
        remote(dst, dst, ss, rs, along(0, 0, 1)).wait_recv()

    def chunk(half, dp, dq):
        return pl.ds(half * 64 + dp * 16 + dq * 4, 4)

    c_qown.wait()
    for axis in (0, 1):
        for k in (2, 1, 3):
            for half in (0, 1):
                back = (4 - k) % 4
                send(
                    qown.at[pl.ds(4 * half, 4)],
                    qall.at[chunk(half, back, 0) if axis == 0 else chunk(half, 0, back)],
                    gs.at[half, axis * 3 + k - 1],
                    gr.at[half, back, 0] if axis == 0 else gr.at[half, 0, back],
                    along(half, axis, k),
                )
    own_copies = []
    for half in (0, 1):
        copy = pltpu.make_async_copy(qown.at[pl.ds(4 * half, 4)], qall.at[chunk(half, 0, 0)], qsem.at[half])
        copy.start()
        own_copies.append(copy)
    c_tk, c_tv = local_copy(1, tk_hbm, tkb), local_copy(2, tv_hbm, tvb)
    c_nk, c_nv = local_copy(3, nk_hbm, nkb), local_copy(4, nv_hbm, nvb)
    c_w = local_copy(7, w_hbm, wb)

    def gathered(half, dp, dq):
        received(qall.at[chunk(half, dp, dq)], gs.at[half, 0], gr.at[half, dp, dq])

    def forward(dp):
        for half in (0, 1):
            gathered(half, dp, 0)
            for k in (2, 1, 3):
                to = qall.at[chunk(half, dp, (4 - k) % 4)]
                send(qall.at[chunk(half, dp, 0)], to, gs.at[half, 3 + dp * 3 + k - 1], gr.at[half, dp, (4 - k) % 4], along(half, 1, k))

    c_sr.wait()
    c_tl.wait()
    lane8 = iota((8, 128), 1)
    at_slot = jnp.full((8, 128), -1, I32)
    slot_of = jnp.zeros((8, 128), I32)
    for j in range(SLOTS):
        request = sr[j]
        home, half, fourth = request // 8, (request % 8) // 4, request % 4
        dz, dx = (home // 4 - z + 4) % 4, (home % 4 - x + 4) % 4
        position = half * 64 + jnp.where(half == 0, dz * 4 + dx, dx * 4 + dz) * 4 + fourth
        at_slot = jnp.where(lane8 == j, position, at_slot)
        slot_of = jnp.where(lane8 == position, j, slot_of)
    ivec[...] = slot_of
    c_inv = pltpu.make_async_copy(ivec, inv, lsem.at[8])
    c_inv.start()
    here = (jnp.broadcast_to(at_slot[0:1], (REQ, 128)) == iota((REQ, 128), 0)).astype(F32)
    absent[...] = jnp.broadcast_to((1.0 - jnp.sum(here, axis=1, keepdims=True)) * VERY_LOW, (REQ, 128))
    l1[...] = jnp.zeros_like(l1)
    lloc[...] = jnp.zeros_like(lloc)

    def home_part():
        c_tk.wait()
        c_tv.wait()
        c_nk.wait()
        c_nv.wait()
        new_scores = lax.dot_general(qown[...].reshape(OWN * R, HD), nkb[...], NT, preferred_element_type=F32)
        token = iota((R, 256), 1)
        new_lane, step = iota((R, 32), 1), iota((R, 32), 0) // 8
        lane, log_columns = iota((R, 128), 1), jnp.zeros((R, 128), F32)
        for r in range(OWN):
            old = lax.dot_general(qown[r], tkb[r], NT, preferred_element_type=F32)
            old = jnp.where(token < tl[r], old, VERY_LOW)
            new = new_scores[r * R : (r + 1) * R]
            new = jnp.where((new_lane >= 4 * r) & (new_lane <= 4 * r + step), new, VERY_LOW)
            peak = jnp.maximum(jnp.max(old, axis=1, keepdims=True), jnp.max(new, axis=1, keepdims=True))
            old = jnp.exp2((old - peak) * SCALE2)
            new = jnp.exp2((new - peak) * SCALE2)
            total = jnp.sum(old, axis=1, keepdims=True) + jnp.sum(new, axis=1, keepdims=True)
            result = jnp.dot(old.astype(BF16), tvb[r], preferred_element_type=F32)
            result = result + jnp.dot(new.astype(BF16), nvb[...], preferred_element_type=F32)
            lo[r] = (result * (1.0 / total)).astype(BF16)
            log_columns = jnp.where(lane == r, peak * SCALE2 + jnp.log2(total), log_columns)
        pick = (iota((OWN, 128), 0) == iota((OWN, 128), 1)).astype(F32).astype(BF16)
        rows = to_rows(pick, log_columns)
        lloc[0, 0:4] = rows[0:4]
        lloc[1, 0:4] = rows[4:8]

    def lend(chunks):
        lane, zeros = iota((R, 128), 1), jnp.zeros((R, HD), BF16)
        todo = []
        for half, dp, dq in chunks:
            todo += [((half, dp), half * 64 + dp * 16 + dq * 4 + i, dq * 4 + i) for i in (0, 2)]
        log_columns = {}
        for half, dp, _ in chunks:
            if (half, dp) not in log_columns:
                log_columns[half, dp] = logs_of[half, dp]
        slots = [[inv[0, first + u] for u in (0, 1)] for _, first, _ in todo]
        scores = []
        for (_, first, _), (a, b) in zip(todo, slots):
            queries = [qall[first + u] for u in (0, 1)]
            queries = [jnp.concatenate([queries[0], zeros], axis=1), jnp.concatenate([zeros, queries[1]], axis=1)]
            keys = jnp.concatenate([kb[a], kb[b]], axis=1)
            scores.append(lax.dot_general(jnp.concatenate(queries, axis=0), keys, NT, preferred_element_type=F32))
        peaks = [jnp.max(score, axis=1, keepdims=True) for score in scores]
        terms = [jnp.exp2((score - peak) * SCALE2) for score, peak in zip(scores, peaks)]
        totals = [jnp.sum(term, axis=1, keepdims=True) for term in terms]
        for (key, first, column), (a, b), peak, term, total in zip(todo, slots, peaks, terms, totals):
            values = jnp.concatenate([vb[a], vb[b]], axis=1)
            result = jnp.dot(term.astype(BF16), values, preferred_element_type=F32)
            inverse = 1.0 / total
            logs = peak * SCALE2 + jnp.log2(total)
            omsg[first] = (result[:R, :HD] * inverse[:R]).astype(BF16)
            omsg[first + 1] = (result[R:, HD:] * inverse[R:]).astype(BF16)
            log_columns[key] = jnp.where(lane == column, logs[:R], log_columns[key])
            log_columns[key] = jnp.where(lane == column + 1, logs[R:], log_columns[key])
        for key in log_columns:
            logs_of[key] = log_columns[key]

    def send_line(dp):
        pick = (iota((16, 128), 0) == iota((16, 128), 1)).astype(F32).astype(BF16)
        for half in (0, 1):
            send_part(half, dp, EARLY if dp in (1, 3) else 0, 16)
        for half in (0, 1):
            part = pl.ds(half * 64 + dp * 16, 16)
            lmsg[part] = to_rows(pick, logs_of[half, dp]) + absent[part]
            if dp:
                send(lmsg.at[part], rl1.at[half, dp - 1], s1.at[half, dp - 1, 2], r1.at[half, dp - 1, 2], along(half, 0, dp))
        if dp == 2 and EARLY:
            for half in (0, 1):
                for other in (3, 1):
                    send_part(half, other, 0, EARLY)

    def send_part(half, dp, start, end):
        if dp:
            send(
                omsg.at[pl.ds(half * 64 + dp * 16 + start, end - start)],
                ro1.at[half, dp - 1, pl.ds(start, end - start)],
                s1.at[half, dp - 1, int(start > 0)],
                r1.at[half, dp - 1, int(start > 0)],
                along(half, 0, dp),
            )

    def first_merge(half):
        base = half * 64
        for k in FIRST:
            received(rl1.at[half, k - 1], s1.at[half, 0, 0], r1.at[half, k - 1, 2])
        weights, log = merge_weights([lmsg[pl.ds(base, 16)]] + [rl1[half, k] for k in range(3)])
        weights = by_lane_group(weights)
        for i in range(4):
            l1[half, i, 0:4] = log[4 * i : 4 * i + 4]
        for k in FIRST:
            for start, end in ((0, EARLY), (EARLY, 16)) if EARLY and k != 2 else ((0, 16),):
                received(ro1.at[half, k - 1, pl.ds(start, end - start)], s1.at[half, 0, 0], r1.at[half, k - 1, int(start > 0)])

        def merge(k):
            parts = [[omsg[base + k * 4 + u]] + [ro1[half, n, k * 4 + u] for n in range(3)] for u in range(4)]
            for u, result in enumerate(scaled_sums(weights[k * 4 : k * 4 + 4], parts)):
                m1[half, k * 4 + u] = result.astype(BF16)

        for k in (2, 1, 3):
            to = along(half, 1, k)
            send(l1.at[half, k], rl2.at[half, k - 1], s2.at[half, k - 1, 0], r2.at[half, k - 1, 0], to)
            merge(k)
            send(m1.at[half, pl.ds(k * 4, 4)], ro2.at[half, k - 1], s2.at[half, k - 1, 1], r2.at[half, k - 1, 1], to)
        return merge

    def second_merge(half):
        for k in (1, 3, 2):
            received(rl2.at[half, k - 1], s2.at[half, 0, 0], r2.at[half, k - 1, 0])
        weights, _ = merge_weights([l1[half, 0]] + [rl2[half, k] for k in range(3)] + [lloc[half]])
        lent, home = by_lane_group(weights[:4]), weights[4]
        lane, row = iota((R, 128), 1), iota((R, 128), 0)
        picked = [
            jnp.where(lane == row + u * R, jnp.broadcast_to(home[u : u + 1], (R, 128)), 0.0).astype(BF16) for u in range(4)
        ]
        homes = jnp.concatenate([lo[half * 4 + u] for u in range(4)], axis=0)
        own = jnp.dot(jnp.concatenate(picked, axis=0), homes, preferred_element_type=F32)
        for k in (1, 3, 2):
            received(ro2.at[half, k - 1], s2.at[half, 0, 0], r2.at[half, k - 1, 1])
        parts = [[m1[half, u]] + [ro2[half, k, u] for k in range(3)] for u in range(4)]
        for u, result in enumerate(scaled_sums(lent[0:4], parts)):
            att[(half * 4 + u) * R : (half * 4 + u + 1) * R] = result + own[u * R : (u + 1) * R]

    for dp in FORWARD:
        forward(dp)
    c_inv.wait()
    for copy in own_copies:
        copy.wait()
    logs_of = {(half, dp): jnp.zeros((R, 128), F32) for half in (0, 1) for dp in range(4)}
    c_k.wait()
    c_v.wait()
    seen = {0: 0, 1: 0, 2: 0, 3: 0}
    for pairs in GROUPS:
        chunks = [(half, dp, dq) for dp, dq in pairs for half in (0, 1)]
        for half, dp, dq in chunks:
            if dq:
                gathered(half, dp, dq)
        lend(chunks)
        for dp, dq in pairs:
            seen[dp] += 1
        for dp in sorted({dp for dp, _ in pairs if seen[dp] == 4}):
            send_line(dp)
    home_part()
    lent = sent[GATHER:]
    del sent[GATHER:]
    all_sent()
    own_merges = [first_merge(half) for half in (0, 1)]
    for merge in own_merges:
        merge(0)
    for copy in lent:
        copy.wait_send()
    for half in (0, 1):
        second_merge(half)

    flat = jnp.concatenate([att[pl.ds(h, R, stride=8)].astype(BF16) for h in range(8)], axis=1)
    c_w.wait()

    def columns(target, start=0, width=1024):
        at = pl.multiple_of(target * 1024 + start, 512)
        return jnp.dot(flat, wb[:, pl.ds(at, width)], preferred_element_type=F32)

    def share(dy):
        cs[dy] = columns(((y + dy) % 4) * 2 + 1 - c).astype(BF16)
        send(cs.at[dy], cr.at[dy], css.at[dy], crs.at[dy], {"tp": y * 2 + 1 - c})

    def along_y(dy):
        for n in (0, 1):
            value = columns(((y + dy) % 4) * 2 + c, n * 512, 512)
            if n == 0:
                received(cr.at[dy], css.at[dy], crs.at[dy])
            ys[dy - 1, n] = (value + cr[dy, :, n * 512 : (n + 1) * 512].astype(F32)).astype(BF16)
            to = {"tp": ((y + dy) % 4) * 2 + c}
            send(ys.at[dy - 1, n], yr.at[dy - 1, n], yss.at[dy - 1, n], yrs.at[dy - 1, n], to)

    share(2)
    share(1)
    share(3)
    along_y(2)
    along_y(1)
    along_y(3)
    share(0)
    value = columns(y * 2 + c)
    received(cr.at[0], css.at[0], crs.at[0])
    value = value + cr[0].astype(F32)
    last = sent[-7:]
    del sent[-7:]
    all_sent()
    for dy in (2, 1, 3):
        for n in (0, 1):
            received(yr.at[dy - 1, n], yss.at[dy - 1, n], yrs.at[dy - 1, n])
        value = value + jnp.concatenate([yr[dy - 1, 0], yr[dy - 1, 1]], axis=1).astype(F32)
    out[...] = value.astype(BF16)
    for copy in last:
        copy.wait_send()


def per_device(
    queries, tail_keys, tail_values, new_keys, new_values, tail_lengths, pool_keys, pool_values, slot_request, out_weight
):
    in_hbm = pl.BlockSpec(memory_space=pltpu.HBM)
    dma = pltpu.SemaphoreType.DMA

    def v(*shape, dtype=BF16):
        return pltpu.VMEM(shape, dtype)

    args = (
        slot_request,
        tail_lengths,
        queries.reshape(OWN, R, HD),
        tail_keys.reshape(OWN, 256, HD),
        tail_values.reshape(OWN, 256, HD),
        new_keys.reshape(R, HD),
        new_values.reshape(R, HD),
        pool_keys.reshape(SLOTS, 256, HD),
        pool_values.reshape(SLOTS, 256, HD),
        out_weight,
    )
    result = pl.pallas_call(
        kernel,
        out_shape=jax.ShapeDtypeStruct((R, 1024), BF16),
        in_specs=[in_hbm] * len(args),
        out_specs=pl.BlockSpec(memory_space=pltpu.VMEM),
        scratch_shapes=[
            v(REQ, R, HD), v(OWN, R, HD), v(SLOTS, 256, HD), v(SLOTS, 256, HD), v(OWN, 256, HD), v(OWN, 256, HD),
            v(R, HD), v(R, HD), v(1024, 8192),
            v(REQ, R, HD), v(REQ, 128, dtype=F32), v(REQ, 128, dtype=F32),
            v(2, 3, 16, R, HD), v(2, 3, 16, 128, dtype=F32),
            v(2, 16, R, HD), v(2, 4, 8, 128, dtype=F32),
            v(2, 3, 4, R, HD), v(2, 3, 8, 128, dtype=F32),
            v(OWN, R, HD), v(2, 8, 128, dtype=F32), v(OWN * R, HD, dtype=F32),
            v(4, R, 1024), v(4, R, 1024), v(3, 2, R, 512), v(3, 2, R, 512),
            pltpu.SMEM((SLOTS,), I32), pltpu.SMEM((OWN,), I32), v(8, 128, dtype=I32), pltpu.SMEM((8, 128), I32),
            dma((11,)), dma((2,)), dma((2, 15)), dma((2, 4, 4)),
            dma((2, 3, 3)), dma((2, 3, 3)), dma((2, 3, 2)), dma((2, 3, 2)),
            dma((4,)), dma((4,)), dma((3, 2)), dma((3, 2)),
        ],
        name="lent_attention",
        compiler_params=pltpu.CompilerParams(collective_id=0, has_side_effects=True, vmem_limit_bytes=44 * 2**20),
    )(*[pltpu.with_memory_space_constraint(arg, pltpu.HBM) for arg in args])
    return result.reshape(OWN, 4, 1024)


def solution(mesh):
    placed = (
        P("inst", None, "tp", None),
        P("inst", "tp", None, None),
        P("inst", "tp", None, None),
        P("inst", None, "tp", None),
        P("inst", None, "tp", None),
        P("inst"),
        P("inst", "tp", None, None),
        P("inst", "tp", None, None),
        P("inst"),
        P("tp", None),
    )
    return jax.shard_map(
        per_device, mesh=mesh, in_specs=placed, out_specs=P("inst", None, "tp"), check_vma=False
    )
```

```python
import functools

import jax
import jax.numpy as jnp
from jax import lax
from jax.experimental import pallas as pl
from jax.experimental.pallas import tpu as pltpu
from jax.sharding import PartitionSpec as P

MESH = pl.DeviceIdType.MESH
VERY_LOW = -1e30
HD = 128
LOG2E = 1.4426950408889634
SCALE2 = HD**-0.5 * LOG2E
NT = (((1,), (1,)), ((), ()))
F32, BF16, I32 = jnp.float32, jnp.bfloat16, jnp.int32

SLOTS = 48
OWN = 8
REQ = 128
R = 32
GROUPS = (
    ((0, 0), (0, 1), (0, 3), (0, 2)),
    ((2, 0), (3, 0), (1, 0)),
    ((2, 1), (2, 3), (2, 2)),
    ((3, 1), (3, 3), (3, 2)),
    ((1, 1), (1, 3), (1, 2)),
)
EARLY = 4
GATHER = 30
FORWARD = (2, 3, 1)
FIRST = (2, 1, 3)


def remote(src, dst, send_sem, recv_sem, device):
    return pltpu.make_async_remote_copy(
        src_ref=src, dst_ref=dst, send_sem=send_sem, recv_sem=recv_sem, device_id=device, device_id_type=MESH
    )


def iota(shape, dim):
    return lax.broadcasted_iota(I32, shape, dim)


def to_rows(one_hot, columns):
    copies = jnp.concatenate([columns] * (128 // R), axis=0)
    high = copies.astype(BF16)
    rest = copies - high.astype(F32)
    middle = rest.astype(BF16)
    low = (rest - middle.astype(F32)).astype(BF16)
    parts = [lax.dot_general(one_hot, part, NT, preferred_element_type=F32) for part in (high, middle, low)]
    return parts[0] + parts[1] + parts[2]


def scaled_sums(weights, parts):
    lane, row = iota((R, 128), 1), iota((R, 128), 0)
    diagonal = lane % R == row
    zeros = jnp.zeros((R, 128), BF16)
    picked = [jnp.where(diagonal, jnp.broadcast_to(weights[i : i + 1], (R, 128)), 0.0).astype(BF16) for i in range(4)]
    rows = [jnp.concatenate([zeros, pick] if i % 2 else [pick, zeros], axis=1) for i, pick in enumerate(picked)]
    left = jnp.concatenate(parts[0] + parts[1], axis=0)
    right = jnp.concatenate(parts[2] + parts[3], axis=0)
    result = jnp.dot(jnp.concatenate(rows, axis=0), jnp.concatenate([left, right], axis=1), preferred_element_type=F32)
    return [result[i * R : (i + 1) * R, (i // 2) * 128 : (i // 2 + 1) * 128] for i in range(4)]


def merge_weights(logs):
    top = functools.reduce(jnp.maximum, logs)
    terms = [jnp.exp2(log - top) for log in logs]
    total = functools.reduce(jnp.add, terms)
    inverse = 1.0 / total
    return [term * inverse for term in terms], top + jnp.log2(total)


def by_lane_group(weights):
    group = iota(weights[0].shape, 1) // R
    result = weights[0]
    for k in range(1, len(weights)):
        result = jnp.where(group == k, weights[k], result)
    return result


def kernel(
    sr_hbm, tl_hbm, q_hbm, tk_hbm, tv_hbm, nk_hbm, nv_hbm, pk_hbm, pv_hbm, w_hbm,
    out,
    qall, qown, kb, vb, tkb, tvb, nkb, nvb, wb,
    omsg, lmsg, absent, ro1, rl1, m1, l1, ro2, rl2, lo, lloc, att, cs, cr, ys, yr,
    sr, tl, ivec, inv,
    lsem, qsem, gs, gr, s1, r1, s2, r2, css, crs, yss, yrs,
):
    inst, tp = lax.axis_index("inst"), lax.axis_index("tp")
    z, x, y, c = inst // 4, inst % 4, tp // 2, tp % 2

    def along(half, axis, k):
        if (axis == 0) == (half == 0):
            return {"inst": ((z + k) % 4) * 4 + x}
        return {"inst": z * 4 + (x + k) % 4}

    barrier = pltpu.get_barrier_semaphore()
    peers = [along(0, axis, k) for axis in (0, 1) for k in (2, 1, 3)]
    peers += [{"tp": ((y + k) % 4) * 2 + c} for k in (2, 1, 3)] + [{"tp": y * 2 + 1 - c}]
    for peer in peers:
        pl.semaphore_signal(barrier, inc=1, device_id=peer, device_id_type=MESH)

    def local_copy(i, src, dst):
        copy = pltpu.make_async_copy(src, dst, lsem.at[i])
        copy.start()
        return copy

    c_sr, c_tl = local_copy(9, sr_hbm, sr), local_copy(10, tl_hbm, tl)
    c_qown = local_copy(0, q_hbm, qown)
    c_k, c_v = local_copy(5, pk_hbm, kb), local_copy(6, pv_hbm, vb)
    pl.semaphore_wait(barrier, len(peers))

    sent = []

    def send(src, dst, ss, rs, device):
        copy = remote(src, dst, ss, rs, device)
        copy.start()
        sent.append(copy)

    def all_sent():
        for copy in sent:
            copy.wait_send()
        del sent[:]

    def received(dst, ss, rs):
        remote(dst, dst, ss, rs, along(0, 0, 1)).wait_recv()

    def chunk(half, dp, dq):
        return pl.ds(half * 64 + dp * 16 + dq * 4, 4)

    c_qown.wait()
    for axis in (0, 1):
        for k in (2, 1, 3):
            for half in (0, 1):
                back = (4 - k) % 4
                send(
                    qown.at[pl.ds(4 * half, 4)],
                    qall.at[chunk(half, back, 0) if axis == 0 else chunk(half, 0, back)],
                    gs.at[half, axis * 3 + k - 1],
                    gr.at[half, back, 0] if axis == 0 else gr.at[half, 0, back],
                    along(half, axis, k),
                )
    own_copies = []
    for half in (0, 1):
        copy = pltpu.make_async_copy(qown.at[pl.ds(4 * half, 4)], qall.at[chunk(half, 0, 0)], qsem.at[half])
        copy.start()
        own_copies.append(copy)
    c_tk, c_tv = local_copy(1, tk_hbm, tkb), local_copy(2, tv_hbm, tvb)
    c_nk, c_nv = local_copy(3, nk_hbm, nkb), local_copy(4, nv_hbm, nvb)
    c_w = local_copy(7, w_hbm, wb)

    def gathered(half, dp, dq):
        received(qall.at[chunk(half, dp, dq)], gs.at[half, 0], gr.at[half, dp, dq])

    def forward(dp):
        for half in (0, 1):
            gathered(half, dp, 0)
            for k in (2, 1, 3):
                to = qall.at[chunk(half, dp, (4 - k) % 4)]
                send(qall.at[chunk(half, dp, 0)], to, gs.at[half, 3 + dp * 3 + k - 1], gr.at[half, dp, (4 - k) % 4], along(half, 1, k))

    c_sr.wait()
    c_tl.wait()
    lane8 = iota((8, 128), 1)
    at_slot = jnp.full((8, 128), -1, I32)
    slot_of = jnp.zeros((8, 128), I32)
    for j in range(SLOTS):
        request = sr[j]
        home, half, fourth = request // 8, (request % 8) // 4, request % 4
        dz, dx = (home // 4 - z + 4) % 4, (home % 4 - x + 4) % 4
        position = half * 64 + jnp.where(half == 0, dz * 4 + dx, dx * 4 + dz) * 4 + fourth
        at_slot = jnp.where(lane8 == j, position, at_slot)
        slot_of = jnp.where(lane8 == position, j, slot_of)
    ivec[...] = slot_of
    c_inv = pltpu.make_async_copy(ivec, inv, lsem.at[8])
    c_inv.start()
    here = (jnp.broadcast_to(at_slot[0:1], (REQ, 128)) == iota((REQ, 128), 0)).astype(F32)
    absent[...] = jnp.broadcast_to((1.0 - jnp.sum(here, axis=1, keepdims=True)) * VERY_LOW, (REQ, 128))
    l1[...] = jnp.zeros_like(l1)
    lloc[...] = jnp.zeros_like(lloc)

    def home_part():
        c_tk.wait()
        c_tv.wait()
        c_nk.wait()
        c_nv.wait()
        new_scores = lax.dot_general(qown[...].reshape(OWN * R, HD), nkb[...], NT, preferred_element_type=F32)
        token = iota((R, 256), 1)
        new_lane, step = iota((R, 32), 1), iota((R, 32), 0) // 8
        lane, log_columns = iota((R, 128), 1), jnp.zeros((R, 128), F32)
        for r in range(OWN):
            old = lax.dot_general(qown[r], tkb[r], NT, preferred_element_type=F32)
            old = jnp.where(token < tl[r], old, VERY_LOW)
            new = new_scores[r * R : (r + 1) * R]
            new = jnp.where((new_lane >= 4 * r) & (new_lane <= 4 * r + step), new, VERY_LOW)
            peak = jnp.maximum(jnp.max(old, axis=1, keepdims=True), jnp.max(new, axis=1, keepdims=True))
            old = jnp.exp2((old - peak) * SCALE2)
            new = jnp.exp2((new - peak) * SCALE2)
            total = jnp.sum(old, axis=1, keepdims=True) + jnp.sum(new, axis=1, keepdims=True)
            result = jnp.dot(old.astype(BF16), tvb[r], preferred_element_type=F32)
            result = result + jnp.dot(new.astype(BF16), nvb[...], preferred_element_type=F32)
            lo[r] = (result * (1.0 / total)).astype(BF16)
            log_columns = jnp.where(lane == r, peak * SCALE2 + jnp.log2(total), log_columns)
        pick = (iota((OWN, 128), 0) == iota((OWN, 128), 1)).astype(F32).astype(BF16)
        rows = to_rows(pick, log_columns)
        lloc[0, 0:4] = rows[0:4]
        lloc[1, 0:4] = rows[4:8]

    def lend(chunks):
        lane, zeros = iota((R, 128), 1), jnp.zeros((R, HD), BF16)
        todo = []
        for half, dp, dq in chunks:
            todo += [((half, dp), half * 64 + dp * 16 + dq * 4 + i, dq * 4 + i) for i in (0, 2)]
        log_columns = {}
        for half, dp, _ in chunks:
            if (half, dp) not in log_columns:
                log_columns[half, dp] = logs_of[half, dp]
        slots = [[inv[0, first + u] for u in (0, 1)] for _, first, _ in todo]
        scores = []
        for (_, first, _), (a, b) in zip(todo, slots):
            queries = [qall[first + u] for u in (0, 1)]
            queries = [jnp.concatenate([queries[0], zeros], axis=1), jnp.concatenate([zeros, queries[1]], axis=1)]
            keys = jnp.concatenate([kb[a], kb[b]], axis=1)
            scores.append(lax.dot_general(jnp.concatenate(queries, axis=0), keys, NT, preferred_element_type=F32))
        peaks = [jnp.max(score, axis=1, keepdims=True) for score in scores]
        terms = [jnp.exp2((score - peak) * SCALE2) for score, peak in zip(scores, peaks)]
        totals = [jnp.sum(term, axis=1, keepdims=True) for term in terms]
        for (key, first, column), (a, b), peak, term, total in zip(todo, slots, peaks, terms, totals):
            values = jnp.concatenate([vb[a], vb[b]], axis=1)
            result = jnp.dot(term.astype(BF16), values, preferred_element_type=F32)
            inverse = 1.0 / total
            logs = peak * SCALE2 + jnp.log2(total)
            omsg[first] = (result[:R, :HD] * inverse[:R]).astype(BF16)
            omsg[first + 1] = (result[R:, HD:] * inverse[R:]).astype(BF16)
            log_columns[key] = jnp.where(lane == column, logs[:R], log_columns[key])
            log_columns[key] = jnp.where(lane == column + 1, logs[R:], log_columns[key])
        for key in log_columns:
            logs_of[key] = log_columns[key]

    def send_line(dp):
        pick = (iota((16, 128), 0) == iota((16, 128), 1)).astype(F32).astype(BF16)
        for half in (0, 1):
            send_part(half, dp, EARLY if dp in (1, 3) else 0, 16)
        for half in (0, 1):
            part = pl.ds(half * 64 + dp * 16, 16)
            lmsg[part] = to_rows(pick, logs_of[half, dp]) + absent[part]
            if dp:
                send(lmsg.at[part], rl1.at[half, dp - 1], s1.at[half, dp - 1, 2], r1.at[half, dp - 1, 2], along(half, 0, dp))
        if dp == 2 and EARLY:
            for half in (0, 1):
                for other in (3, 1):
                    send_part(half, other, 0, EARLY)

    def send_part(half, dp, start, end):
        if dp:
            send(
                omsg.at[pl.ds(half * 64 + dp * 16 + start, end - start)],
                ro1.at[half, dp - 1, pl.ds(start, end - start)],
                s1.at[half, dp - 1, int(start > 0)],
                r1.at[half, dp - 1, int(start > 0)],
                along(half, 0, dp),
            )

    def first_merge(half):
        base = half * 64
        for k in FIRST:
            received(rl1.at[half, k - 1], s1.at[half, 0, 0], r1.at[half, k - 1, 2])
        weights, log = merge_weights([lmsg[pl.ds(base, 16)]] + [rl1[half, k] for k in range(3)])
        weights = by_lane_group(weights)
        for i in range(4):
            l1[half, i, 0:4] = log[4 * i : 4 * i + 4]
        for k in FIRST:
            for start, end in ((0, EARLY), (EARLY, 16)) if EARLY and k != 2 else ((0, 16),):
                received(ro1.at[half, k - 1, pl.ds(start, end - start)], s1.at[half, 0, 0], r1.at[half, k - 1, int(start > 0)])

        def merge(k):
            parts = [[omsg[base + k * 4 + u]] + [ro1[half, n, k * 4 + u] for n in range(3)] for u in range(4)]
            for u, result in enumerate(scaled_sums(weights[k * 4 : k * 4 + 4], parts)):
                m1[half, k * 4 + u] = result.astype(BF16)

        for k in (2, 1, 3):
            to = along(half, 1, k)
            send(l1.at[half, k], rl2.at[half, k - 1], s2.at[half, k - 1, 0], r2.at[half, k - 1, 0], to)
            merge(k)
            send(m1.at[half, pl.ds(k * 4, 4)], ro2.at[half, k - 1], s2.at[half, k - 1, 1], r2.at[half, k - 1, 1], to)
        return merge

    def second_merge(half):
        for k in (1, 3, 2):
            received(rl2.at[half, k - 1], s2.at[half, 0, 0], r2.at[half, k - 1, 0])
        weights, _ = merge_weights([l1[half, 0]] + [rl2[half, k] for k in range(3)] + [lloc[half]])
        lent, home = by_lane_group(weights[:4]), weights[4]
        lane, row = iota((R, 128), 1), iota((R, 128), 0)
        picked = [
            jnp.where(lane == row + u * R, jnp.broadcast_to(home[u : u + 1], (R, 128)), 0.0).astype(BF16) for u in range(4)
        ]
        homes = jnp.concatenate([lo[half * 4 + u] for u in range(4)], axis=0)
        own = jnp.dot(jnp.concatenate(picked, axis=0), homes, preferred_element_type=F32)
        for k in (1, 3, 2):
            received(ro2.at[half, k - 1], s2.at[half, 0, 0], r2.at[half, k - 1, 1])
        parts = [[m1[half, u]] + [ro2[half, k, u] for k in range(3)] for u in range(4)]
        for u, result in enumerate(scaled_sums(lent[0:4], parts)):
            att[(half * 4 + u) * R : (half * 4 + u + 1) * R] = result + own[u * R : (u + 1) * R]

    for dp in FORWARD:
        forward(dp)
    c_inv.wait()
    for copy in own_copies:
        copy.wait()
    logs_of = {(half, dp): jnp.zeros((R, 128), F32) for half in (0, 1) for dp in range(4)}
    c_k.wait()
    c_v.wait()
    seen = {0: 0, 1: 0, 2: 0, 3: 0}
    for pairs in GROUPS:
        chunks = [(half, dp, dq) for dp, dq in pairs for half in (0, 1)]
        for half, dp, dq in chunks:
            if dq:
                gathered(half, dp, dq)
        lend(chunks)
        for dp, dq in pairs:
            seen[dp] += 1
        for dp in sorted({dp for dp, _ in pairs if seen[dp] == 4}):
            send_line(dp)
    home_part()
    lent = sent[GATHER:]
    del sent[GATHER:]
    all_sent()
    own_merges = [first_merge(half) for half in (0, 1)]
    for merge in own_merges:
        merge(0)
    for copy in lent:
        copy.wait_send()
    for half in (0, 1):
        second_merge(half)

    flat = jnp.concatenate([att[pl.ds(h, R, stride=8)].astype(BF16) for h in range(8)], axis=1)
    c_w.wait()

    def columns(target, start=0, width=1024):
        at = pl.multiple_of(target * 1024 + start, 512)
        return jnp.dot(flat, wb[:, pl.ds(at, width)], preferred_element_type=F32)

    def share(dy):
        cs[dy] = columns(((y + dy) % 4) * 2 + 1 - c).astype(BF16)
        send(cs.at[dy], cr.at[dy], css.at[dy], crs.at[dy], {"tp": y * 2 + 1 - c})

    def along_y(*pieces):
        for dy, n in pieces:
            value = columns(((y + dy) % 4) * 2 + c, n * 512, 512)
            if n == 0:
                received(cr.at[dy], css.at[dy], crs.at[dy])
            ys[dy - 1, n] = (value + cr[dy, :, n * 512 : (n + 1) * 512].astype(F32)).astype(BF16)
            to = {"tp": ((y + dy) % 4) * 2 + c}
            send(ys.at[dy - 1, n], yr.at[dy - 1, n], yss.at[dy - 1, n], yrs.at[dy - 1, n], to)

    share(2)
    share(1)
    share(3)
    along_y((2, 0), (2, 1), (1, 0), (3, 0), (1, 1), (3, 1))
    share(0)
    value = columns(y * 2 + c)
    received(cr.at[0], css.at[0], crs.at[0])
    value = value + cr[0].astype(F32)
    last = sent[-7:]
    del sent[-7:]
    all_sent()
    for dy in (2, 1, 3):
        for n in (0, 1):
            received(yr.at[dy - 1, n], yss.at[dy - 1, n], yrs.at[dy - 1, n])
        value = value + jnp.concatenate([yr[dy - 1, 0], yr[dy - 1, 1]], axis=1).astype(F32)
    out[...] = value.astype(BF16)
    for copy in last:
        copy.wait_send()


def per_device(
    queries, tail_keys, tail_values, new_keys, new_values, tail_lengths, pool_keys, pool_values, slot_request, out_weight
):
    in_hbm = pl.BlockSpec(memory_space=pltpu.HBM)
    dma = pltpu.SemaphoreType.DMA

    def v(*shape, dtype=BF16):
        return pltpu.VMEM(shape, dtype)

    args = (
        slot_request,
        tail_lengths,
        queries.reshape(OWN, R, HD),
        tail_keys.reshape(OWN, 256, HD),
        tail_values.reshape(OWN, 256, HD),
        new_keys.reshape(R, HD),
        new_values.reshape(R, HD),
        pool_keys.reshape(SLOTS, 256, HD),
        pool_values.reshape(SLOTS, 256, HD),
        out_weight,
    )
    result = pl.pallas_call(
        kernel,
        out_shape=jax.ShapeDtypeStruct((R, 1024), BF16),
        in_specs=[in_hbm] * len(args),
        out_specs=pl.BlockSpec(memory_space=pltpu.VMEM),
        scratch_shapes=[
            v(REQ, R, HD), v(OWN, R, HD), v(SLOTS, 256, HD), v(SLOTS, 256, HD), v(OWN, 256, HD), v(OWN, 256, HD),
            v(R, HD), v(R, HD), v(1024, 8192),
            v(REQ, R, HD), v(REQ, 128, dtype=F32), v(REQ, 128, dtype=F32),
            v(2, 3, 16, R, HD), v(2, 3, 16, 128, dtype=F32),
            v(2, 16, R, HD), v(2, 4, 8, 128, dtype=F32),
            v(2, 3, 4, R, HD), v(2, 3, 8, 128, dtype=F32),
            v(OWN, R, HD), v(2, 8, 128, dtype=F32), v(OWN * R, HD, dtype=F32),
            v(4, R, 1024), v(4, R, 1024), v(3, 2, R, 512), v(3, 2, R, 512),
            pltpu.SMEM((SLOTS,), I32), pltpu.SMEM((OWN,), I32), v(8, 128, dtype=I32), pltpu.SMEM((8, 128), I32),
            dma((11,)), dma((2,)), dma((2, 15)), dma((2, 4, 4)),
            dma((2, 3, 3)), dma((2, 3, 3)), dma((2, 3, 2)), dma((2, 3, 2)),
            dma((4,)), dma((4,)), dma((3, 2)), dma((3, 2)),
        ],
        name="lent_attention",
        compiler_params=pltpu.CompilerParams(collective_id=0, has_side_effects=True, vmem_limit_bytes=44 * 2**20),
    )(*[pltpu.with_memory_space_constraint(arg, pltpu.HBM) for arg in args])
    return result.reshape(OWN, 4, 1024)


def solution(mesh):
    placed = (
        P("inst", None, "tp", None),
        P("inst", "tp", None, None),
        P("inst", "tp", None, None),
        P("inst", None, "tp", None),
        P("inst", None, "tp", None),
        P("inst"),
        P("inst", "tp", None, None),
        P("inst", "tp", None, None),
        P("inst"),
        P("tp", None),
    )
    return jax.shard_map(
        per_device, mesh=mesh, in_specs=placed, out_specs=P("inst", None, "tp"), check_vma=False
    )
```
